128 devices in a mesh: dom: 64 (over z, y, x), st: 2 (over core).
Axes of the slice: x: 4, y: 4, z: 4, core: 2. Of those that a mesh axis runs over, the one named last changes fastest.
Arguments:
- states: float32 [32, 64, 24, 24, 128], P('st', 'dom'), may hold values from -20 to 20
- potential: float32 [64, 24, 24, 128], P('dom'), may hold values from 0.5 to 8
Outputs:
- filtered: float32 [32, 64, 24, 24, 128], P('st', 'dom')
- gram: float32 [32, 32], P('st')
The draws below stay inside these ranges and needn't reach their ends.
All inputs are finite; a program needn't handle non-finite values.
Results may differ from the reference program's by a relative error of at most 0.00005.
Values sent between devices are 32-bit elements; how exact they have to be, the bound alone decides.
A program may use at most 64 MiB of HBM per device.

```python
import math
import jax
import jax.numpy as jnp
from jax import lax

NST = 32
PY = 8
CX = 24
CY = 24
NZ = 128
NX = 192
NY = 192
N_DOM = 64


def draw_states(key, part):
    key = jax.random.fold_in(key, 1)
    first_key = jax.random.fold_in(key, 0)
    second_key = jax.random.fold_in(key, 1)
    fourth_key = jax.random.fold_in(key, 3)
    position = jnp.arange(N_DOM, dtype=jnp.float32) / max(N_DOM - 1, 1)
    rising = (1.0 + 2.0 * position).reshape(1, N_DOM, 1, 1, 1)
    weights = jax.random.uniform(fourth_key, (NST, 1, 1, 1, 1), jnp.float32, -0.5, 0.5)
    noise = jnp.clip(jax.random.normal(first_key, (NST, N_DOM, CX, CY, NZ), jnp.float32), -4.0, 4.0)
    common = jnp.clip(jax.random.normal(second_key, (1, N_DOM, CX, CY, NZ), jnp.float32), -4.0, 4.0)
    return noise * rising + weights * common * rising


def shard_levels(stream_key, dims, shards, least, top_value):
    level = 1.0
    for axis_at, shards_of in shards:
        draws = jax.random.uniform(jax.random.fold_in(jax.random.fold_in(stream_key, 6), axis_at), (shards_of,), jnp.float32, least / len(shards), top_value / len(shards))
        level = level * jnp.repeat(jnp.exp(draws), dims[axis_at] // shards_of).reshape((-1,) + (1,) * (len(dims) - 1 - axis_at))
    return level


def setup_inputs(seed: int = 0) -> dict:
    streams_of = jax.random.split(jax.random.key(seed), 3)
    return {
        "states": draw_states(jax.random.fold_in(streams_of[2], 71), 0),
        "potential": jnp.clip(jnp.exp(math.log(8.0) - 2.7725887 * jax.random.uniform(streams_of[1], (N_DOM, CX, CY, NZ), jnp.float32) ** shard_levels(streams_of[1], (N_DOM, CX, CY, NZ), ((0, 64),), -0.2, 0.2)), 0.5, 8.0),
    }


COEFFS = (-5369.0 / 1800.0, 12.0 / 7.0, -15.0 / 56.0, 10.0 / 189.0, -1.0 / 112.0, 2.0 / 1925.0, -1.0 / 16632.0)


def to_grid(blocks):
    count, sizex, sizey, sizez = blocks.shape
    rows = count // PY
    return blocks.reshape(rows, PY, sizex, sizey, sizez).transpose(0, 2, 1, 3, 4).reshape(rows * sizex, PY * sizey, sizez)


def from_grid(field, sizex, sizey):
    lenx, leny, lenz = field.shape
    rows = lenx // sizex
    return field.reshape(rows, sizex, PY, sizey, lenz).transpose(0, 2, 1, 3, 4).reshape(rows * PY, sizex, sizey, lenz)


def hamiltonian(field, potential):
    lenx, leny, lenz = field.shape
    padded = jnp.pad(field, 6)
    laplace = 3.0 * COEFFS[0] * field
    for offset in range(1, 7):
        beside_all = padded[6 + offset:6 + offset + lenx, 6:6 + leny, 6:6 + lenz] + padded[6 - offset:6 - offset + lenx, 6:6 + leny, 6:6 + lenz]
        beside_all = beside_all + padded[6:6 + lenx, 6 + offset:6 + offset + leny, 6:6 + lenz] + padded[6:6 + lenx, 6 - offset:6 - offset + leny, 6:6 + lenz]
        beside_all = beside_all + padded[6:6 + lenx, 6:6 + leny, 6 + offset:6 + offset + lenz] + padded[6:6 + lenx, 6:6 + leny, 6 - offset:6 - offset + lenz]
        laplace = laplace + COEFFS[offset] * beside_all
    return -0.5 / 0.25 * laplace + potential * field


def filter_state(blocks, potential_grid):
    field = to_grid(blocks)
    first = (hamiltonian(field, potential_grid) - 36.0 * field) / 32.0
    result = 2.0 * (hamiltonian(first, potential_grid) - 36.0 * first) / 32.0 - field
    return from_grid(result, CX, CY)


def reference(states, potential):
    potential_grid = to_grid(potential)
    filtered = lax.map(lambda blocks: filter_state(blocks, potential_grid), states)
    flat = filtered.reshape(NST, -1)
    gram = jnp.einsum("sc,tc->st", flat, flat, precision=lax.Precision.HIGHEST) / (NX * NY * NZ)
    return filtered, gram
```

```python
import functools

import jax
import jax.numpy as jnp
from jax import lax
from jax.experimental import pallas as pl
from jax.experimental.pallas import tpu as pltpu
from jax.sharding import PartitionSpec as P

COEFFS = (
    -5369.0 / 1800.0,
    12.0 / 7.0,
    -15.0 / 56.0,
    10.0 / 189.0,
    -1.0 / 112.0,
    2.0 / 1925.0,
    -1.0 / 16632.0,
)
SCALED = tuple(-2.0 * c / 32.0 for c in COEFFS)
PY = 8
HALO = 6
EDGE = 8
HIGHEST = lax.Precision.HIGHEST


def band_matrix(size):
    row = lax.broadcasted_iota(jnp.int32, (size, size), 0)
    column = lax.broadcasted_iota(jnp.int32, (size, size), 1)
    distance = jnp.abs(row - column)
    band = jnp.zeros((size, size), jnp.float32)
    for offset in range(1, HALO + 1):
        band = jnp.where(distance == offset, SCALED[offset], band)
    return band


def kernel(
    states, potential, filtered, gram,
    field, first, mate, diagonal, along_z, band, partial_own, partial_mate, sums_y, sums_x,
    load_sem, send1, recv1, send2, recv2, mate_send, mate_recv, store_sem, sum_send, sum_recv,
):
    count, _, sizex, sizey, sizez = states.shape
    rows = lax.axis_size("dom") // PY
    dom = lax.axis_index("dom")
    core = lax.axis_index("st")
    bx, by = dom // PY, dom % PY
    inx = pl.ds(HALO, sizex)
    iny = pl.ds(EDGE, sizey)

    links = (
        (bx < rows - 1, dom + PY, bx > 0, (pl.ds(sizex - HALO, HALO), pl.ds(0, sizey)), (pl.ds(0, HALO), iny)),
        (bx > 0, dom - PY, bx < rows - 1, (pl.ds(0, HALO), pl.ds(0, sizey)), (pl.ds(HALO + sizex, HALO), iny)),
        (by < PY - 1, dom + 1, by > 0, (pl.ds(0, sizex), pl.ds(sizey - EDGE, EDGE)), (inx, pl.ds(0, EDGE))),
        (by > 0, dom - 1, by < PY - 1, (pl.ds(0, sizex), pl.ds(0, EDGE)), (inx, pl.ds(EDGE + sizey, EDGE))),
    )

    barrier = pltpu.get_barrier_semaphore()
    for has_target, target, _, _, _ in links:
        @pl.when(has_target)
        def _():
            pl.semaphore_signal(barrier, inc=1, device_id={"dom": target}, device_id_type=pl.DeviceIdType.MESH)
    pl.semaphore_signal(barrier, inc=1, device_id={"st": 1 - core}, device_id_type=pl.DeviceIdType.MESH)
    for other in range(1, PY):
        near = bx * PY + lax.rem(by + other, PY)
        far = lax.rem(bx + other, rows) * PY + by
        pl.semaphore_signal(barrier, inc=1, device_id={"dom": near}, device_id_type=pl.DeviceIdType.MESH)
        pl.semaphore_signal(barrier, inc=1, device_id={"dom": far}, device_id_type=pl.DeviceIdType.MESH)

    def load(s):
        return pltpu.make_async_copy(states.at[s, 0], field.at[s, inx, iny], load_sem.at[s])

    def halo(s, link, source, landing, send_sem, recv_sem):
        _, target, _, taken, placed = links[link]
        return pltpu.make_async_remote_copy(
            src_ref=source(s, taken),
            dst_ref=landing.at[s, placed[0], placed[1]],
            send_sem=send_sem.at[s, link],
            recv_sem=recv_sem.at[s, link],
            device_id={"dom": target},
            device_id_type=pl.DeviceIdType.MESH,
        )

    def halo1(s, link):
        return halo(s, link, lambda s, taken: states.at[s, 0, taken[0], taken[1]], field, send1, recv1)

    def halo2(s, link):
        def source(s, taken):
            return first.at[s, pl.ds(HALO + taken[0].start, taken[0].size), pl.ds(EDGE + taken[1].start, taken[1].size)]
        return halo(s, link, source, first, send2, recv2)

    def start_all(s, copies):
        for link in range(4):
            @pl.when(links[link][0])
            def _():
                copies(s, link).start()

    def wait_sent(s, copies):
        for link in range(4):
            @pl.when(links[link][0])
            def _():
                copies(s, link).wait_send()

    def wait_landed(s, copies):
        for link in range(4):
            @pl.when(links[link][2])
            def _():
                copies(s, link).wait_recv()

    def start_loads(s, carry):
        load(s).start()
        return carry

    lax.fori_loop(0, count, start_loads, 0)

    def clear(s, carry):
        for link in range(4):
            placed = links[link][4]

            @pl.when(jnp.logical_not(links[link][2]))
            def _():
                zero = jnp.zeros((placed[0].size, placed[1].size, sizez), jnp.float32)
                field[s, placed[0], placed[1], :] = zero
                first[s, placed[0], placed[1], :] = zero
        return carry

    neighbours = sum(link[0].astype(jnp.int32) for link in links)
    pl.semaphore_wait(barrier, neighbours + 1 + 2 * (PY - 1))

    def start_first(s, carry):
        start_all(s, halo1)
        return carry

    lax.fori_loop(0, count, start_first, 0)
    lax.fori_loop(0, count, clear, 0)
    band[...] = band_matrix(sizez)
    diagonal[...] = 3.0 * SCALED[0] + (potential[0] - 36.0) / 32.0

    def apply(padded, s, put):
        inner = padded[s, inx, iny, :].reshape(sizex * sizey, sizez)
        along_z[...] = jnp.dot(
            inner, band[...], precision=HIGHEST, preferred_element_type=jnp.float32
        ).reshape(sizex, sizey, sizez)

        def plane(x, carry):
            total = diagonal[x] * padded[s, HALO + x, iny, :] + along_z[x]
            for k in range(1, HALO + 1):
                beside = padded[s, HALO + x + k, iny, :] + padded[s, HALO + x - k, iny, :]
                beside = beside + padded[s, HALO + x, pl.ds(EDGE + k, sizey), :]
                beside = beside + padded[s, HALO + x, pl.ds(EDGE - k, sizey), :]
                total = total + SCALED[k] * beside
            put(x, total)
            return carry

        lax.fori_loop(0, sizex, plane, 0)

    def first_step(s, carry):
        load(s).wait()
        wait_landed(s, halo1)

        def put(x, total):
            first[s, HALO + x, iny, :] = total

        apply(field, s, put)
        start_all(s, halo2)
        return carry

    lax.fori_loop(0, count, first_step, 0)

    def to_mate(s):
        return pltpu.make_async_remote_copy(
            src_ref=field.at[s, inx, iny],
            dst_ref=mate.at[s],
            send_sem=mate_send.at[s],
            recv_sem=mate_recv.at[s],
            device_id={"st": 1 - core},
            device_id_type=pl.DeviceIdType.MESH,
        )

    def store(s):
        return pltpu.make_async_copy(field.at[s, inx, iny], filtered.at[s, 0], store_sem.at[s])

    def second_step(s, carry):
        wait_landed(s, halo2)

        def put(x, total):
            field[s, HALO + x, iny, :] = 2.0 * total - field[s, HALO + x, iny, :]

        apply(first, s, put)
        to_mate(s).start()
        store(s).start()
        return carry

    lax.fori_loop(0, count, second_step, 0)

    partial_own[...] = jnp.zeros_like(partial_own)
    partial_mate[...] = jnp.zeros_like(partial_mate)

    def wait_mate(s, carry):
        to_mate(s).wait_recv()
        return carry

    lax.fori_loop(0, count, wait_mate, 0)

    def times(a, b):
        return lax.dot_general(
            a, b, (((1,), (1,)), ((), ())), precision=HIGHEST, preferred_element_type=jnp.float32
        )

    def products(x, carry):
        for group in range(sizey // 8):
            own = field[:, HALO + x, pl.ds(EDGE + 8 * group, 8), :].reshape(count * 8, sizez)
            other = mate[:, x, pl.ds(8 * group, 8), :].reshape(count * 8, sizez)
            partial_own[...] += times(own, own)
            partial_mate[...] += times(own, other)
        return carry

    lax.fori_loop(0, sizex, products, 0)

    pairs = count * 8
    row = lax.broadcasted_iota(jnp.int32, (pairs, pairs), 0)
    column = lax.broadcasted_iota(jnp.int32, (pairs, pairs), 1)
    same = lax.rem(row, 8) == lax.rem(column, 8)
    fold = (
        lax.broadcasted_iota(jnp.int32, (count, pairs), 0)
        == lax.broadcasted_iota(jnp.int32, (count, pairs), 1) // 8
    ).astype(jnp.float32)
    spread_row = lax.broadcasted_iota(jnp.int32, (pairs, 128), 0) // 8
    spread_column = lax.broadcasted_iota(jnp.int32, (pairs, 128), 1)

    def folded(partial, at):
        inner = jnp.dot(fold, jnp.where(same, partial[...], 0.0), precision=HIGHEST, preferred_element_type=jnp.float32)
        spread = (spread_row + at * count == spread_column).astype(jnp.float32)
        return jnp.dot(inner, spread, precision=HIGHEST, preferred_element_type=jnp.float32)

    mine = folded(partial_own, core) + folded(partial_mate, 1 - core)

    def sum_over(stage, buffer, at, position, value):
        buffer[at] = value

        def copy(other):
            return pltpu.make_async_remote_copy(
                src_ref=buffer.at[at],
                dst_ref=buffer.at[at],
                send_sem=sum_send.at[stage, other],
                recv_sem=sum_recv.at[stage, at],
                device_id={"dom": position(lax.rem(at + other, PY))},
                device_id_type=pl.DeviceIdType.MESH,
            )

        def arriving(other):
            source = lax.rem(at + other, PY)
            return pltpu.make_async_remote_copy(
                src_ref=buffer.at[source],
                dst_ref=buffer.at[source],
                send_sem=sum_send.at[stage, other],
                recv_sem=sum_recv.at[stage, source],
                device_id={"dom": position(source)},
                device_id_type=pl.DeviceIdType.MESH,
            )

        for other in range(1, PY):
            copy(other).start()
        for other in range(1, PY):
            arriving(other).wait_recv()
        for other in range(1, PY):
            copy(other).wait_send()
        total = buffer[0]
        for other in range(1, PY):
            total = total + buffer[other]
        return total

    row_sum = sum_over(0, sums_y, by, lambda at: bx * PY + at, mine)
    whole = sum_over(1, sums_x, bx, lambda at: at * PY + by, row_sum)
    cells = lax.axis_size("dom") * sizex * sizey * sizez
    gram[...] = whole[:, : gram.shape[1]] / cells

    def finish(s, carry):
        wait_sent(s, halo1)
        wait_sent(s, halo2)
        to_mate(s).wait_send()
        store(s).wait()
        return carry

    lax.fori_loop(0, count, finish, 0)


def on_device(states, potential):
    count, _, sizex, sizey, sizez = states.shape
    padded = (count, sizex + 2 * HALO, sizey + 2 * EDGE, sizez)
    dma = pltpu.SemaphoreType.DMA
    return pl.pallas_call(
        kernel,
        out_shape=(
            jax.ShapeDtypeStruct(states.shape, jnp.float32),
            jax.ShapeDtypeStruct((count, 2 * count), jnp.float32),
        ),
        in_specs=[pl.BlockSpec(memory_space=pl.ANY), pl.BlockSpec(memory_space=pltpu.VMEM)],
        out_specs=(pl.BlockSpec(memory_space=pl.ANY), pl.BlockSpec(memory_space=pltpu.VMEM)),
        scratch_shapes=[
            pltpu.VMEM(padded, jnp.float32),
            pltpu.VMEM(padded, jnp.float32),
            pltpu.VMEM((count, sizex, sizey, sizez), jnp.float32),
            pltpu.VMEM((sizex, sizey, sizez), jnp.float32),
            pltpu.VMEM((sizex, sizey, sizez), jnp.float32),
            pltpu.VMEM((sizez, sizez), jnp.float32),
            pltpu.VMEM((count * 8, count * 8), jnp.float32),
            pltpu.VMEM((count * 8, count * 8), jnp.float32),
            pltpu.VMEM((PY, count, 128), jnp.float32),
            pltpu.VMEM((PY, count, 128), jnp.float32),
            dma((count,)),
            dma((count, 4)),
            dma((count, 4)),
            dma((count, 4)),
            dma((count, 4)),
            dma((count,)),
            dma((count,)),
            dma((count,)),
            dma((2, PY)),
            dma((2, PY)),
        ],
        compiler_params=pltpu.CompilerParams(
            collective_id=0, has_side_effects=True, vmem_limit_bytes=50 * 2**20
        ),
        name="chebyshev",
    )(states, potential)


def solution(mesh):
    in_specs = (P("st", "dom", None, None, None), P("dom", None, None, None))
    out_specs = (P("st", "dom", None, None, None), P("st", None))
    return jax.shard_map(
        on_device, mesh=mesh, in_specs=in_specs, out_specs=out_specs, check_vma=False
    )
```

```python
import functools

import jax
import jax.numpy as jnp
from jax import lax
from jax.experimental import pallas as pl
from jax.experimental.pallas import tpu as pltpu
from jax.sharding import PartitionSpec as P

COEFFS = (
    -5369.0 / 1800.0,
    12.0 / 7.0,
    -15.0 / 56.0,
    10.0 / 189.0,
    -1.0 / 112.0,
    2.0 / 1925.0,
    -1.0 / 16632.0,
)
SCALED = tuple(-2.0 * c / 32.0 for c in COEFFS)
PY = 8
COLUMNS = 4
AHEAD = 10
RELAYED = 5
HALO = 6
EDGE = 8
HIGHEST = lax.Precision.HIGHEST


def band_matrix(size):
    row = lax.broadcasted_iota(jnp.int32, (size, size), 0)
    column = lax.broadcasted_iota(jnp.int32, (size, size), 1)
    distance = jnp.abs(row - column)
    band = jnp.zeros((size, size), jnp.float32)
    for offset in range(1, HALO + 1):
        band = jnp.where(distance == offset, SCALED[offset], band)
    return band


def pick(chosen, yes, no):
    chosen = chosen.astype(jnp.int32)
    return chosen * yes + (1 - chosen) * no


def kernel(
    states, potential, filtered, gram,
    field, first, mate, diagonal, along_z, band, partial_own, partial_mate, sums_y, sums_x,
    box_x1, box_y1, box_x2, box_y2,
    load_sem, send1, recv1, part_send1, part_recv1, relay_send1, relay_recv1,
    send2, recv2, part_send2, part_recv2, relay_send2, relay_recv2, mate_send, mate_recv, store_sem, sum_send, sum_recv,
):
    count, _, sizex, sizey, sizez = states.shape
    rows = lax.axis_size("dom") // PY
    dom = lax.axis_index("dom")
    core = lax.axis_index("st")
    bx, by = dom // PY, dom % PY
    inx = pl.ds(HALO, sizex)
    iny = pl.ds(EDGE, sizey)

    links = (
        (bx < rows - 1, dom + PY, bx > 0, (pl.ds(sizex - HALO, HALO), pl.ds(0, sizey)), (pl.ds(0, HALO), iny)),
        (bx > 0, dom - PY, bx < rows - 1, (pl.ds(0, HALO), pl.ds(0, sizey)), (pl.ds(HALO + sizex, HALO), iny)),
        (by < PY - 1, dom + 1, by > 0, (pl.ds(0, sizex), pl.ds(sizey - HALO, HALO)), (inx, pl.ds(EDGE - HALO, HALO))),
        (by > 0, dom - 1, by < PY - 1, (pl.ds(0, sizex), pl.ds(0, HALO)), (inx, pl.ds(EDGE + sizey, HALO))),
    )

    level = bx // 2
    odd = bx % 2 == 1
    outward = 2 * PY * (2 * (bx % 2) - 1)
    direct = pick(odd, 3 - level, level)
    outer = jnp.logical_and(bx > 0, bx < rows - 1)
    relays_x = pick(odd, level, 3 - level) > 0
    relayed_from = pick(odd, 4 - level, level + 1)

    def detours(s):
        return jnp.logical_and(outer, s % 4 >= direct)

    def relays(s):
        return jnp.logical_and(relays_x, s % 4 >= relayed_from)

    my_column = by % COLUMNS
    upper = by >= COLUMNS
    crosses = jnp.logical_or(by == COLUMNS - 1, by == COLUMNS)
    relays_y = jnp.logical_not(crosses)
    across = pick(upper, 0, COLUMNS)
    end = pick(upper, COLUMNS, COLUMNS - 1)
    part = sizex // COLUMNS

    barrier = pltpu.get_barrier_semaphore()
    pl.semaphore_signal(barrier, inc=1, device_id={"st": 1 - core}, device_id_type=pl.DeviceIdType.MESH)
    for other in range(1, PY):
        near = bx * PY + lax.rem(by + other, PY)
        far = lax.rem(bx + other, rows) * PY + by
        pl.semaphore_signal(barrier, inc=1, device_id={"dom": near}, device_id_type=pl.DeviceIdType.MESH)
        pl.semaphore_signal(barrier, inc=1, device_id={"dom": far}, device_id_type=pl.DeviceIdType.MESH)

    def load(s):
        return pltpu.make_async_copy(states.at[s, 0], field.at[s, inx, iny], load_sem.at[s])

    def remote(src, dst, send_sem, recv_sem, target):
        return pltpu.make_async_remote_copy(
            src_ref=src,
            dst_ref=dst,
            send_sem=send_sem,
            recv_sem=recv_sem,
            device_id={"dom": target},
            device_id_type=pl.DeviceIdType.MESH,
        )

    class Exchange:
        def __init__(self, source, landing, box_x, box_y, sems):
            self.source, self.landing, self.box_x, self.box_y = source, landing, box_x, box_y
            self.send, self.recv, self.part_send, self.part_recv, self.relay_send, self.relay_recv = sems

        def face(self, s, link):
            _, target, _, taken, placed = links[link]
            return remote(
                self.source(s, taken), self.landing.at[s, placed[0], placed[1]],
                self.send.at[s, link], self.recv.at[s, link], target,
            )

        def face_by_relay(self, s, link):
            _, _, _, taken, _ = links[link]
            return remote(
                self.source(s, taken), self.box_x.at[s], self.send.at[s, link], self.relay_recv.at[s, 0], dom + outward
            )

        def hand_on_face(self, s, link):
            placed = links[link][4]
            return remote(
                self.box_x.at[s], self.landing.at[s, placed[0], placed[1]],
                self.relay_send.at[s, 0], self.recv.at[s, link], dom - outward // 2,
            )

        def piece(self, s, link, at):
            _, _, _, taken, placed = links[link]
            return remote(
                self.source(s, (pl.ds(at * part, part), taken[1])),
                self.landing.at[s, pl.ds(HALO + at * part, part), placed[1]],
                self.part_send.at[s, at], self.part_recv.at[s, at], bx * PY + across + at,
            )

        def piece_by_relay(self, s, link, at):
            taken = links[link][3]
            return remote(
                self.source(s, (pl.ds(at * part, part), taken[1])), self.box_y.at[s, :, pl.ds(0, HALO)],
                self.part_send.at[s, at], self.relay_recv.at[s, 1], bx * PY + across + at,
            )

        def hand_on_piece(self, s, link):
            placed = links[link][4]
            return remote(
                self.box_y.at[s, :, pl.ds(0, HALO)],
                self.landing.at[s, pl.ds(HALO + my_column * part, part), placed[1]],
                self.relay_send.at[s, 1], self.part_recv.at[s].at[my_column], bx * PY + end,
            )

        def for_faces(self, s, act, by_relay):
            for link in (0, 1):
                outermost = odd if link == 0 else jnp.logical_not(odd)
                turns = jnp.logical_and(outermost, detours(s))

                @pl.when(jnp.logical_and(links[link][0], jnp.logical_not(turns)))
                def _():
                    act(self.face(s, link))

                @pl.when(jnp.logical_and(links[link][0], turns))
                def _():
                    act(by_relay(s, link))
            for link, at in ((2, COLUMNS - 1), (3, COLUMNS)):
                @pl.when(jnp.logical_and(links[link][0], by != at))
                def _():
                    act(self.face(s, link))

                @pl.when(by == at)
                def _():
                    for piece in range(COLUMNS):
                        straight = piece == (0 if link == 2 else COLUMNS - 1)
                        act((self.piece if straight else self.piece_by_relay)(s, link, piece))

        def start(self, s):
            self.for_faces(s, lambda copy: copy.start(), self.face_by_relay)

        def wait_sent(self, s):
            self.for_faces(s, lambda copy: copy.wait_send(), self.face_by_relay)
            self.for_relays(s, None, lambda copy: copy.wait_send())

        def for_relays(self, s, arrived, act):
            for link, mine in ((0, odd), (1, jnp.logical_not(odd))):
                @pl.when(jnp.logical_and(mine, relays(s)))
                def _():
                    if arrived is not None:
                        arrived(self.face_by_relay(s, link))
                    act(self.hand_on_face(s, link))
            for link, mine in ((2, upper), (3, jnp.logical_not(upper))):
                @pl.when(jnp.logical_and(mine, relays_y))
                def _():
                    if arrived is not None:
                        arrived(self.piece_by_relay(s, link, 0))
                    act(self.hand_on_piece(s, link))

        def hand_on(self, s):
            self.for_relays(s, lambda copy: copy.wait_recv(), lambda copy: copy.start())

        def wait_landed(self, s):
            for link in (0, 1):
                @pl.when(links[link][2])
                def _():
                    self.face(s, link).wait_recv()
            for link, at in ((2, COLUMNS), (3, COLUMNS - 1)):
                @pl.when(jnp.logical_and(links[link][2], by != at))
                def _():
                    self.face(s, link).wait_recv()

                @pl.when(by == at)
                def _():
                    for piece in range(COLUMNS):
                        self.piece(s, link, piece).wait_recv()

    def from_first(s, taken):
        return first.at[s, pl.ds(HALO + taken[0].start, taken[0].size), pl.ds(EDGE + taken[1].start, taken[1].size)]

    exchange1 = Exchange(
        lambda s, taken: states.at[s, 0, taken[0], taken[1]], field, box_x1, box_y1,
        (send1, recv1, part_send1, part_recv1, relay_send1, relay_recv1),
    )
    exchange2 = Exchange(
        from_first, first, box_x2, box_y2, (send2, recv2, part_send2, part_recv2, relay_send2, relay_recv2)
    )

    def start_loads(s, carry):
        load(s).start()
        return carry

    lax.fori_loop(0, count, start_loads, 0)

    def clear(s, carry):
        for link in range(4):
            placed = links[link][4]

            @pl.when(jnp.logical_not(links[link][2]))
            def _():
                zero = jnp.zeros((placed[0].size, placed[1].size, sizez), jnp.float32)
                field[s, placed[0], placed[1], :] = zero
                first[s, placed[0], placed[1], :] = zero
        return carry

    pl.semaphore_wait(barrier, 1 + 2 * (PY - 1))

    def start_first(s, carry):
        exchange1.start(s)
        return carry

    lax.fori_loop(0, AHEAD, start_first, 0)
    lax.fori_loop(0, count, clear, 0)
    band[...] = band_matrix(sizez)
    diagonal[...] = 3.0 * SCALED[0] + (potential[0] - 36.0) / 32.0

    def apply(padded, s, put):
        inner = padded[s, inx, iny, :].reshape(sizex * sizey, sizez)
        along_z[...] = jnp.dot(
            inner, band[...], precision=HIGHEST, preferred_element_type=jnp.float32
        ).reshape(sizex, sizey, sizez)

        def plane(x, carry):
            total = diagonal[x] * padded[s, HALO + x, iny, :] + along_z[x]
            for k in range(1, HALO + 1):
                beside = padded[s, HALO + x + k, iny, :] + padded[s, HALO + x - k, iny, :]
                beside = beside + padded[s, HALO + x, pl.ds(EDGE + k, sizey), :]
                beside = beside + padded[s, HALO + x, pl.ds(EDGE - k, sizey), :]
                total = total + SCALED[k] * beside
            put(x, total)
            return carry

        lax.fori_loop(0, sizex, plane, 0)

    def hand_on_ahead(exchange, s):
        @pl.when(s == 0)
        def _():
            for early in range(RELAYED):
                exchange.hand_on(early)

        @pl.when(s + RELAYED < count)
        def _():
            exchange.hand_on(s + RELAYED)

    def first_step(s, carry):
        @pl.when(s + AHEAD < count)
        def _():
            exchange1.start(s + AHEAD)

        hand_on_ahead(exchange1, s)
        load(s).wait()
        exchange1.wait_landed(s)

        def put(x, total):
            first[s, HALO + x, iny, :] = total

        apply(field, s, put)
        exchange2.start(s)
        return carry

    lax.fori_loop(0, count, first_step, 0)

    def to_mate(s):
        return pltpu.make_async_remote_copy(
            src_ref=field.at[s, inx, iny],
            dst_ref=mate.at[s],
            send_sem=mate_send.at[s],
            recv_sem=mate_recv.at[s],
            device_id={"st": 1 - core},
            device_id_type=pl.DeviceIdType.MESH,
        )

    def store(s):
        return pltpu.make_async_copy(field.at[s, inx, iny], filtered.at[s, 0], store_sem.at[s])

    def second_step(s, carry):
        hand_on_ahead(exchange2, s)
        exchange2.wait_landed(s)

        def put(x, total):
            field[s, HALO + x, iny, :] = 2.0 * total - field[s, HALO + x, iny, :]

        apply(first, s, put)
        to_mate(s).start()
        store(s).start()
        return carry

    lax.fori_loop(0, count, second_step, 0)

    partial_own[...] = jnp.zeros_like(partial_own)
    partial_mate[...] = jnp.zeros_like(partial_mate)

    def wait_mate(s, carry):
        to_mate(s).wait_recv()
        return carry

    lax.fori_loop(0, count, wait_mate, 0)

    def times(a, b):
        return lax.dot_general(
            a, b, (((1,), (1,)), ((), ())), precision=HIGHEST, preferred_element_type=jnp.float32
        )

    def products(x, carry):
        for group in range(sizey // 8):
            own = field[:, HALO + x, pl.ds(EDGE + 8 * group, 8), :].reshape(count * 8, sizez)
            other = mate[:, x, pl.ds(8 * group, 8), :].reshape(count * 8, sizez)
            partial_own[...] += times(own, own)
            partial_mate[...] += times(own, other)
        return carry

    lax.fori_loop(0, sizex, products, 0)

    pairs = count * 8
    row = lax.broadcasted_iota(jnp.int32, (pairs, pairs), 0)
    column = lax.broadcasted_iota(jnp.int32, (pairs, pairs), 1)
    same = lax.rem(row, 8) == lax.rem(column, 8)
    fold = (
        lax.broadcasted_iota(jnp.int32, (count, pairs), 0)
        == lax.broadcasted_iota(jnp.int32, (count, pairs), 1) // 8
    ).astype(jnp.float32)
    spread_row = lax.broadcasted_iota(jnp.int32, (pairs, 128), 0) // 8
    spread_column = lax.broadcasted_iota(jnp.int32, (pairs, 128), 1)

    def folded(partial, at):
        inner = jnp.dot(fold, jnp.where(same, partial[...], 0.0), precision=HIGHEST, preferred_element_type=jnp.float32)
        spread = (spread_row + at * count == spread_column).astype(jnp.float32)
        return jnp.dot(inner, spread, precision=HIGHEST, preferred_element_type=jnp.float32)

    mine = folded(partial_own, core) + folded(partial_mate, 1 - core)

    def sum_over(stage, buffer, at, position, value):
        buffer[at] = value

        def copy(other):
            return pltpu.make_async_remote_copy(
                src_ref=buffer.at[at],
                dst_ref=buffer.at[at],
                send_sem=sum_send.at[stage, other],
                recv_sem=sum_recv.at[stage, at],
                device_id={"dom": position(lax.rem(at + other, PY))},
                device_id_type=pl.DeviceIdType.MESH,
            )

        def arriving(other):
            source = lax.rem(at + other, PY)
            return pltpu.make_async_remote_copy(
                src_ref=buffer.at[source],
                dst_ref=buffer.at[source],
                send_sem=sum_send.at[stage, other],
                recv_sem=sum_recv.at[stage, source],
                device_id={"dom": position(source)},
                device_id_type=pl.DeviceIdType.MESH,
            )

        for other in range(1, PY):
            copy(other).start()
        for other in range(1, PY):
            arriving(other).wait_recv()
        for other in range(1, PY):
            copy(other).wait_send()
        total = buffer[0]
        for other in range(1, PY):
            total = total + buffer[other]
        return total

    row_sum = sum_over(0, sums_y, by, lambda at: bx * PY + at, mine)
    whole = sum_over(1, sums_x, bx, lambda at: at * PY + by, row_sum)
    cells = lax.axis_size("dom") * sizex * sizey * sizez
    gram[...] = whole[:, : gram.shape[1]] / cells

    def finish(s, carry):
        exchange1.wait_sent(s)
        exchange2.wait_sent(s)
        to_mate(s).wait_send()
        store(s).wait()
        return carry

    lax.fori_loop(0, count, finish, 0)


def on_device(states, potential):
    count, _, sizex, sizey, sizez = states.shape
    padded = (count, sizex + 2 * HALO, sizey + 2 * EDGE, sizez)
    dma = pltpu.SemaphoreType.DMA
    return pl.pallas_call(
        kernel,
        out_shape=(
            jax.ShapeDtypeStruct(states.shape, jnp.float32),
            jax.ShapeDtypeStruct((count, 2 * count), jnp.float32),
        ),
        in_specs=[pl.BlockSpec(memory_space=pl.ANY), pl.BlockSpec(memory_space=pltpu.VMEM)],
        out_specs=(pl.BlockSpec(memory_space=pl.ANY), pl.BlockSpec(memory_space=pltpu.VMEM)),
        scratch_shapes=[
            pltpu.VMEM(padded, jnp.float32),
            pltpu.VMEM(padded, jnp.float32),
            pltpu.VMEM((count, sizex, sizey, sizez), jnp.float32),
            pltpu.VMEM((sizex, sizey, sizez), jnp.float32),
            pltpu.VMEM((sizex, sizey, sizez), jnp.float32),
            pltpu.VMEM((sizez, sizez), jnp.float32),
            pltpu.VMEM((count * 8, count * 8), jnp.float32),
            pltpu.VMEM((count * 8, count * 8), jnp.float32),
            pltpu.VMEM((PY, count, 128), jnp.float32),
            pltpu.VMEM((PY, count, 128), jnp.float32),
            pltpu.VMEM((count, HALO, sizey, sizez), jnp.float32),
            pltpu.VMEM((count, sizex // COLUMNS, 8, sizez), jnp.float32),
            pltpu.VMEM((count, HALO, sizey, sizez), jnp.float32),
            pltpu.VMEM((count, sizex // COLUMNS, 8, sizez), jnp.float32),
            dma((count,)),
        ]
        + 2 * [
            dma((count, 4)),
            dma((count, 4)),
            dma((count, COLUMNS)),
            dma((count, COLUMNS)),
            dma((count, 2)),
            dma((count, 2)),
        ]
        + [
            dma((count,)),
            dma((count,)),
            dma((count,)),
            dma((2, PY)),
            dma((2, PY)),
        ],
        compiler_params=pltpu.CompilerParams(
            collective_id=0, has_side_effects=True, vmem_limit_bytes=50 * 2**20
        ),
        name="chebyshev",
    )(states, potential)


def solution(mesh):
    in_specs = (P("st", "dom", None, None, None), P("dom", None, None, None))
    out_specs = (P("st", "dom", None, None, None), P("st", None))
    return jax.shard_map(
        on_device, mesh=mesh, in_specs=in_specs, out_specs=out_specs, check_vma=False
    )
```

```python
import functools

import jax
import jax.numpy as jnp
from jax import lax
from jax.experimental import pallas as pl
from jax.experimental.pallas import tpu as pltpu
from jax.sharding import PartitionSpec as P

COEFFS = (
    -5369.0 / 1800.0,
    12.0 / 7.0,
    -15.0 / 56.0,
    10.0 / 189.0,
    -1.0 / 112.0,
    2.0 / 1925.0,
    -1.0 / 16632.0,
)
SCALED = tuple(-2.0 * c / 32.0 for c in COEFFS)
PY = 8
COLUMNS = 4
AHEAD = 10
GROUP = 4
PLANES = 8
RELAYED = 5
HALO = 6
EDGE = 8
HIGHEST = lax.Precision.HIGHEST


def band_matrix(size):
    row = lax.broadcasted_iota(jnp.int32, (size, size), 0)
    column = lax.broadcasted_iota(jnp.int32, (size, size), 1)
    distance = jnp.abs(row - column)
    band = jnp.zeros((size, size), jnp.float32)
    for offset in range(1, HALO + 1):
        band = jnp.where(distance == offset, SCALED[offset], band)
    return band


def pick(chosen, yes, no):
    chosen = chosen.astype(jnp.int32)
    return chosen * yes + (1 - chosen) * no


def kernel(
    states, potential, filtered, gram,
    field, first, mate, diagonal, along_z, band, partial, gram_sum, sums_y, sums_x,
    box_x1, box_y1, box_x2, box_y2,
    load_sem, send1, recv1, part_send1, part_recv1, relay_send1, relay_recv1,
    send2, recv2, part_send2, part_recv2, relay_send2, relay_recv2, mate_send, mate_recv, store_sem, sum_send, sum_recv,
):
    count, _, sizex, sizey, sizez = states.shape
    rows = lax.axis_size("dom") // PY
    dom = lax.axis_index("dom")
    core = lax.axis_index("st")
    bx, by = dom // PY, dom % PY
    inx = pl.ds(HALO, sizex)
    iny = pl.ds(EDGE, sizey)

    links = (
        (bx < rows - 1, dom + PY, bx > 0, (pl.ds(sizex - HALO, HALO), pl.ds(0, sizey)), (pl.ds(0, HALO), iny)),
        (bx > 0, dom - PY, bx < rows - 1, (pl.ds(0, HALO), pl.ds(0, sizey)), (pl.ds(HALO + sizex, HALO), iny)),
        (by < PY - 1, dom + 1, by > 0, (pl.ds(0, sizex), pl.ds(sizey - HALO, HALO)), (inx, pl.ds(EDGE - HALO, HALO))),
        (by > 0, dom - 1, by < PY - 1, (pl.ds(0, sizex), pl.ds(0, HALO)), (inx, pl.ds(EDGE + sizey, HALO))),
    )

    level = bx // 2
    odd = bx % 2 == 1
    outward = 2 * PY * (2 * (bx % 2) - 1)
    direct = pick(odd, 3 - level, level)
    outer = jnp.logical_and(bx > 0, bx < rows - 1)
    relays_x = pick(odd, level, 3 - level) > 0
    relayed_from = pick(odd, 4 - level, level + 1)

    def detours(s):
        return jnp.logical_and(outer, s % 4 >= direct)

    def relays(s):
        return jnp.logical_and(relays_x, s % 4 >= relayed_from)

    my_column = by % COLUMNS
    upper = by >= COLUMNS
    crosses = jnp.logical_or(by == COLUMNS - 1, by == COLUMNS)
    relays_y = jnp.logical_not(crosses)
    across = pick(upper, 0, COLUMNS)
    end = pick(upper, COLUMNS, COLUMNS - 1)
    part = sizex // COLUMNS

    barrier = pltpu.get_barrier_semaphore()
    pl.semaphore_signal(barrier, inc=1, device_id={"st": 1 - core}, device_id_type=pl.DeviceIdType.MESH)
    for other in range(1, PY):
        near = bx * PY + lax.rem(by + other, PY)
        far = lax.rem(bx + other, rows) * PY + by
        pl.semaphore_signal(barrier, inc=1, device_id={"dom": near}, device_id_type=pl.DeviceIdType.MESH)
        pl.semaphore_signal(barrier, inc=1, device_id={"dom": far}, device_id_type=pl.DeviceIdType.MESH)

    def load(s):
        return pltpu.make_async_copy(states.at[s, 0], field.at[s, inx, iny], load_sem.at[s])

    def remote(src, dst, send_sem, recv_sem, target):
        return pltpu.make_async_remote_copy(
            src_ref=src,
            dst_ref=dst,
            send_sem=send_sem,
            recv_sem=recv_sem,
            device_id={"dom": target},
            device_id_type=pl.DeviceIdType.MESH,
        )

    class Exchange:
        def __init__(self, source, landing, box_x, box_y, sems):
            self.source, self.landing, self.box_x, self.box_y = source, landing, box_x, box_y
            self.send, self.recv, self.part_send, self.part_recv, self.relay_send, self.relay_recv = sems

        def face(self, s, link):
            _, target, _, taken, placed = links[link]
            return remote(
                self.source(s, taken), self.landing.at[s, placed[0], placed[1]],
                self.send.at[s, link], self.recv.at[s, link], target,
            )

        def face_by_relay(self, s, link):
            _, _, _, taken, _ = links[link]
            return remote(
                self.source(s, taken), self.box_x.at[s], self.send.at[s, link], self.relay_recv.at[s, 0], dom + outward
            )

        def hand_on_face(self, s, link):
            placed = links[link][4]
            return remote(
                self.box_x.at[s], self.landing.at[s, placed[0], placed[1]],
                self.relay_send.at[s, 0], self.recv.at[s, link], dom - outward // 2,
            )

        def piece(self, s, link, at):
            _, _, _, taken, placed = links[link]
            return remote(
                self.source(s, (pl.ds(at * part, part), taken[1])),
                self.landing.at[s, pl.ds(HALO + at * part, part), placed[1]],
                self.part_send.at[s, at], self.part_recv.at[s, at], bx * PY + across + at,
            )

        def piece_by_relay(self, s, link, at):
            taken = links[link][3]
            return remote(
                self.source(s, (pl.ds(at * part, part), taken[1])), self.box_y.at[s, :, pl.ds(0, HALO)],
                self.part_send.at[s, at], self.relay_recv.at[s, 1], bx * PY + across + at,
            )

        def hand_on_piece(self, s, link):
            placed = links[link][4]
            return remote(
                self.box_y.at[s, :, pl.ds(0, HALO)],
                self.landing.at[s, pl.ds(HALO + my_column * part, part), placed[1]],
                self.relay_send.at[s, 1], self.part_recv.at[s].at[my_column], bx * PY + end,
            )

        def for_faces(self, s, act, by_relay):
            for link in (0, 1):
                outermost = odd if link == 0 else jnp.logical_not(odd)
                turns = jnp.logical_and(outermost, detours(s))

                @pl.when(jnp.logical_and(links[link][0], jnp.logical_not(turns)))
                def _():
                    act(self.face(s, link))

                @pl.when(jnp.logical_and(links[link][0], turns))
                def _():
                    act(by_relay(s, link))
            for link, at in ((2, COLUMNS - 1), (3, COLUMNS)):
                @pl.when(jnp.logical_and(links[link][0], by != at))
                def _():
                    act(self.face(s, link))

                @pl.when(by == at)
                def _():
                    for piece in range(COLUMNS):
                        straight = piece == (0 if link == 2 else COLUMNS - 1)
                        act((self.piece if straight else self.piece_by_relay)(s, link, piece))

        def start(self, s):
            self.for_faces(s, lambda copy: copy.start(), self.face_by_relay)

        def wait_sent(self, s):
            self.for_faces(s, lambda copy: copy.wait_send(), self.face_by_relay)
            self.for_relays(s, None, lambda copy: copy.wait_send())

        def for_relays(self, s, arrived, act):
            for link, mine in ((0, odd), (1, jnp.logical_not(odd))):
                @pl.when(jnp.logical_and(mine, relays(s)))
                def _():
                    if arrived is not None:
                        arrived(self.face_by_relay(s, link))
                    act(self.hand_on_face(s, link))
            for link, mine in ((2, upper), (3, jnp.logical_not(upper))):
                @pl.when(jnp.logical_and(mine, relays_y))
                def _():
                    if arrived is not None:
                        arrived(self.piece_by_relay(s, link, 0))
                    act(self.hand_on_piece(s, link))

        def hand_on(self, s):
            self.for_relays(s, lambda copy: copy.wait_recv(), lambda copy: copy.start())

        def wait_landed(self, s):
            for link in (0, 1):
                @pl.when(links[link][2])
                def _():
                    self.face(s, link).wait_recv()
            for link, at in ((2, COLUMNS), (3, COLUMNS - 1)):
                @pl.when(jnp.logical_and(links[link][2], by != at))
                def _():
                    self.face(s, link).wait_recv()

                @pl.when(by == at)
                def _():
                    for piece in range(COLUMNS):
                        self.piece(s, link, piece).wait_recv()

    def from_first(s, taken):
        return first.at[s, pl.ds(HALO + taken[0].start, taken[0].size), pl.ds(EDGE + taken[1].start, taken[1].size)]

    exchange1 = Exchange(
        lambda s, taken: states.at[s, 0, taken[0], taken[1]], field, box_x1, box_y1,
        (send1, recv1, part_send1, part_recv1, relay_send1, relay_recv1),
    )
    exchange2 = Exchange(
        from_first, first, box_x2, box_y2, (send2, recv2, part_send2, part_recv2, relay_send2, relay_recv2)
    )

    def start_loads(s, carry):
        load(s).start()
        return carry

    lax.fori_loop(0, count, start_loads, 0)

    def clear(s, carry):
        for link in range(4):
            placed = links[link][4]

            @pl.when(jnp.logical_not(links[link][2]))
            def _():
                zero = jnp.zeros((placed[0].size, placed[1].size, sizez), jnp.float32)
                field[s, placed[0], placed[1], :] = zero
                first[s, placed[0], placed[1], :] = zero
        return carry

    pl.semaphore_wait(barrier, 1 + 2 * (PY - 1))

    def start_first(s, carry):
        exchange1.start(s)
        return carry

    lax.fori_loop(0, AHEAD, start_first, 0)
    lax.fori_loop(0, count, clear, 0)
    band[...] = band_matrix(sizez)
    diagonal[...] = 3.0 * SCALED[0] + (potential[0] - 36.0) / 32.0

    def apply(padded, s, put):
        inner = padded[s, inx, iny, :].reshape(sizex * sizey, sizez)
        along_z[...] = jnp.dot(
            inner, band[...], precision=HIGHEST, preferred_element_type=jnp.float32
        ).reshape(sizex, sizey, sizez)

        def plane(x, carry):
            total = diagonal[x] * padded[s, HALO + x, iny, :] + along_z[x]
            for k in range(1, HALO + 1):
                beside = padded[s, HALO + x + k, iny, :] + padded[s, HALO + x - k, iny, :]
                beside = beside + padded[s, HALO + x, pl.ds(EDGE + k, sizey), :]
                beside = beside + padded[s, HALO + x, pl.ds(EDGE - k, sizey), :]
                total = total + SCALED[k] * beside
            put(x, total)
            return carry

        lax.fori_loop(0, sizex, plane, 0)

    def hand_on_ahead(exchange, s):
        @pl.when(s == 0)
        def _():
            for early in range(RELAYED):
                exchange.hand_on(early)

        @pl.when(s + RELAYED < count)
        def _():
            exchange.hand_on(s + RELAYED)

    def first_step(s, carry):
        @pl.when(s + AHEAD < count)
        def _():
            exchange1.start(s + AHEAD)

        hand_on_ahead(exchange1, s)
        load(s).wait()
        exchange1.wait_landed(s)

        def put(x, total):
            first[s, HALO + x, iny, :] = total

        apply(field, s, put)
        exchange2.start(s)
        return carry

    lax.fori_loop(0, count, first_step, 0)

    def to_mate(s):
        return pltpu.make_async_remote_copy(
            src_ref=field.at[s, inx, iny],
            dst_ref=mate.at[s],
            send_sem=mate_send.at[s],
            recv_sem=mate_recv.at[s],
            device_id={"st": 1 - core},
            device_id_type=pl.DeviceIdType.MESH,
        )

    def store(s):
        return pltpu.make_async_copy(field.at[s, inx, iny], filtered.at[s, 0], store_sem.at[s])

    def second_step(s, carry):
        hand_on_ahead(exchange2, s)
        exchange2.wait_landed(s)

        def put(x, total):
            field[s, HALO + x, iny, :] = 2.0 * total - field[s, HALO + x, iny, :]

        apply(first, s, put)
        to_mate(s).start()
        store(s).start()
        return carry

    gram_sum[...] = jnp.zeros_like(gram_sum)

    def gram_of(group):
        low, high = group * GROUP, (group + 1) * GROUP
        half = 8 * (high + low)
        total = partial.at[pl.ds(0, 2 * half)]
        total[...] = jnp.zeros_like(total)
        for s in range(low, high):
            to_mate(s).wait_recv()

        def flat(ref, first_state, last_state, x, start):
            return jnp.concatenate(
                [
                    ref[first_state:last_state, x + beyond, pl.ds(start + 8 * tile, 8), :].reshape(-1, sizez)
                    for beyond in range(PLANES)
                    for tile in range(sizey // 8)
                ],
                axis=1,
            )

        def halves(values):
            upper_half = values.astype(jnp.bfloat16)
            return upper_half, (values - upper_half.astype(jnp.float32)).astype(jnp.bfloat16)

        def products(turn, carry):
            x = turn * PLANES
            own = halves(flat(field, 0, high, HALO + x, EDGE))
            new = halves(flat(mate, low, high, x, 0))
            if low:
                old = halves(flat(mate, 0, low, x, 0))
                left = jnp.concatenate([own[0], old[0], own[1], old[1]], axis=0)
            else:
                left = jnp.concatenate(own, axis=0)
            right = jnp.concatenate(
                [own[0][8 * low :], new[0], own[1][8 * low :], new[1]], axis=0
            )
            total[...] += lax.dot_general(
                left, right, (((1,), (1,)), ((), ())), preferred_element_type=jnp.float32
            )
            return carry

        lax.fori_loop(0, sizex // PLANES, products, 0)

        def iota(shape, dimension):
            return lax.broadcasted_iota(jnp.int32, shape, dimension)

        def left_state(index):
            index = index - half * (index >= half).astype(jnp.int32)
            own_state = index < 8 * high
            return (index - 8 * high * (index >= 8 * high).astype(jnp.int32)) // 8, own_state

        def right_state(index):
            index = index % (16 * GROUP)
            own_state = index < 8 * GROUP
            return low + (index % (8 * GROUP)) // 8, own_state

        def lane_of(state, own_state):
            own_state = own_state.astype(jnp.int32)
            return state + count * (own_state * core + (1 - own_state) * (1 - core))

        def dot(left, right):
            return jnp.dot(left, right, precision=HIGHEST, preferred_element_type=jnp.float32)

        wide = 32 * GROUP
        equal_rows = iota((2 * half, wide), 0) % 8 == iota((2 * half, wide), 1) % 8
        values = jnp.where(equal_rows, total[...], 0.0)
        state, own_state = left_state(iota((count, 2 * half), 1))
        rows_of = jnp.logical_and(own_state, state == iota((count, 2 * half), 0)).astype(jnp.float32)
        lane = lane_of(*right_state(iota((wide, 128), 0)))
        lanes_of = (lane == iota((wide, 128), 1)).astype(jnp.float32)
        gram_sum[...] += dot(dot(rows_of, values), lanes_of)
        if low:
            state, own_state = right_state(iota((count, wide), 1))
            rows_of = jnp.logical_and(own_state, state == iota((count, wide), 0)).astype(jnp.float32)
            state, own_state = left_state(iota((2 * half, 128), 0))
            lanes_of = jnp.logical_and(
                state < low, lane_of(state, own_state) == iota((2 * half, 128), 1)
            ).astype(jnp.float32)
            turned = lax.dot_general(
                rows_of, values, (((1,), (1,)), ((), ())), precision=HIGHEST, preferred_element_type=jnp.float32
            )
            gram_sum[...] += dot(turned, lanes_of)

    groups = count // GROUP
    done = 0
    for group in range(groups):
        until = min((group + 1) * GROUP + 1, count)
        lax.fori_loop(done, until, second_step, 0)
        done = until
        gram_of(group)

    mine = gram_sum[...]

    def sum_over(stage, buffer, at, position, value):
        buffer[at] = value

        def copy(other):
            return pltpu.make_async_remote_copy(
                src_ref=buffer.at[at],
                dst_ref=buffer.at[at],
                send_sem=sum_send.at[stage, other],
                recv_sem=sum_recv.at[stage, at],
                device_id={"dom": position(lax.rem(at + other, PY))},
                device_id_type=pl.DeviceIdType.MESH,
            )

        def arriving(other):
            source = lax.rem(at + other, PY)
            return pltpu.make_async_remote_copy(
                src_ref=buffer.at[source],
                dst_ref=buffer.at[source],
                send_sem=sum_send.at[stage, other],
                recv_sem=sum_recv.at[stage, source],
                device_id={"dom": position(source)},
                device_id_type=pl.DeviceIdType.MESH,
            )

        for other in range(1, PY):
            copy(other).start()
        for other in range(1, PY):
            arriving(other).wait_recv()
        for other in range(1, PY):
            copy(other).wait_send()
        total = buffer[0]
        for other in range(1, PY):
            total = total + buffer[other]
        return total

    row_sum = sum_over(0, sums_y, by, lambda at: bx * PY + at, mine)
    whole = sum_over(1, sums_x, bx, lambda at: at * PY + by, row_sum)
    cells = lax.axis_size("dom") * sizex * sizey * sizez
    gram[...] = whole[:, : gram.shape[1]] / cells

    def finish(s, carry):
        exchange1.wait_sent(s)
        exchange2.wait_sent(s)
        to_mate(s).wait_send()
        store(s).wait()
        return carry

    lax.fori_loop(0, count, finish, 0)


def on_device(states, potential):
    count, _, sizex, sizey, sizez = states.shape
    padded = (count, sizex + 2 * HALO, sizey + 2 * EDGE, sizez)
    dma = pltpu.SemaphoreType.DMA
    return pl.pallas_call(
        kernel,
        out_shape=(
            jax.ShapeDtypeStruct(states.shape, jnp.float32),
            jax.ShapeDtypeStruct((count, 2 * count), jnp.float32),
        ),
        in_specs=[pl.BlockSpec(memory_space=pl.ANY), pl.BlockSpec(memory_space=pltpu.VMEM)],
        out_specs=(pl.BlockSpec(memory_space=pl.ANY), pl.BlockSpec(memory_space=pltpu.VMEM)),
        scratch_shapes=[
            pltpu.VMEM(padded, jnp.float32),
            pltpu.VMEM(padded, jnp.float32),
            pltpu.VMEM((count, sizex, sizey, sizez), jnp.float32),
            pltpu.VMEM((sizex, sizey, sizez), jnp.float32),
            pltpu.VMEM((sizex, sizey, sizez), jnp.float32),
            pltpu.VMEM((sizez, sizez), jnp.float32),
            pltpu.VMEM((16 * (2 * count - GROUP), 32 * GROUP), jnp.float32),
            pltpu.VMEM((count, 128), jnp.float32),
            pltpu.VMEM((PY, count, 128), jnp.float32),
            pltpu.VMEM((PY, count, 128), jnp.float32),
            pltpu.VMEM((count, HALO, sizey, sizez), jnp.float32),
            pltpu.VMEM((count, sizex // COLUMNS, 8, sizez), jnp.float32),
            pltpu.VMEM((count, HALO, sizey, sizez), jnp.float32),
            pltpu.VMEM((count, sizex // COLUMNS, 8, sizez), jnp.float32),
            dma((count,)),
        ]
        + 2 * [
            dma((count, 4)),
            dma((count, 4)),
            dma((count, COLUMNS)),
            dma((count, COLUMNS)),
            dma((count, 2)),
            dma((count, 2)),
        ]
        + [
            dma((count,)),
            dma((count,)),
            dma((count,)),
            dma((2, PY)),
            dma((2, PY)),
        ],
        compiler_params=pltpu.CompilerParams(
            collective_id=0, has_side_effects=True, vmem_limit_bytes=50 * 2**20
        ),
        name="chebyshev",
    )(states, potential)


def solution(mesh):
    in_specs = (P("st", "dom", None, None, None), P("dom", None, None, None))
    out_specs = (P("st", "dom", None, None, None), P("st", None))
    return jax.shard_map(
        on_device, mesh=mesh, in_specs=in_specs, out_specs=out_specs, check_vma=False
    )
```

```python
import functools

import jax
import jax.numpy as jnp
from jax import lax
from jax.experimental import pallas as pl
from jax.experimental.pallas import tpu as pltpu
from jax.sharding import PartitionSpec as P

COEFFS = (
    -5369.0 / 1800.0,
    12.0 / 7.0,
    -15.0 / 56.0,
    10.0 / 189.0,
    -1.0 / 112.0,
    2.0 / 1925.0,
    -1.0 / 16632.0,
)
SCALED = tuple(-2.0 * c / 32.0 for c in COEFFS)
PY = 8
COLUMNS = 4
AHEAD = 3
BEHIND = 6
RELAYED2 = 3
GROUP = 4
PLANES = 8
RELAYED = 2
HALO = 6
EDGE = 8
HIGHEST = lax.Precision.HIGHEST


def band_matrix(size):
    row = lax.broadcasted_iota(jnp.int32, (size, size), 0)
    column = lax.broadcasted_iota(jnp.int32, (size, size), 1)
    distance = jnp.abs(row - column)
    band = jnp.zeros((size, size), jnp.float32)
    for offset in range(1, HALO + 1):
        band = jnp.where(distance == offset, SCALED[offset], band)
    return band


def pick(chosen, yes, no):
    chosen = chosen.astype(jnp.int32)
    return chosen * yes + (1 - chosen) * no


def kernel(
    states, potential, filtered, gram,
    field, first, mate, diagonal, along_z, band, partial, gram_sum, sums_y, sums_x,
    box_x1, box_y1, box_x2, box_y2,
    potential_sem, load_sem, send1, recv1, part_send1, part_recv1, relay_send1, relay_recv1,
    send2, recv2, part_send2, part_recv2, relay_send2, relay_recv2, mate_send, mate_recv, sum_send, sum_recv,
):
    count, _, sizex, sizey, sizez = states.shape
    rows = lax.axis_size("dom") // PY
    dom = lax.axis_index("dom")
    core = lax.axis_index("st")
    bx, by = dom // PY, dom % PY
    inx = pl.ds(HALO, sizex)
    iny = pl.ds(EDGE, sizey)

    links = (
        (bx < rows - 1, dom + PY, bx > 0, (pl.ds(sizex - HALO, HALO), pl.ds(0, sizey)), (pl.ds(0, HALO), iny)),
        (bx > 0, dom - PY, bx < rows - 1, (pl.ds(0, HALO), pl.ds(0, sizey)), (pl.ds(HALO + sizex, HALO), iny)),
        (by < PY - 1, dom + 1, by > 0, (pl.ds(0, sizex), pl.ds(sizey - HALO, HALO)), (inx, pl.ds(EDGE - HALO, HALO))),
        (by > 0, dom - 1, by < PY - 1, (pl.ds(0, sizex), pl.ds(0, HALO)), (inx, pl.ds(EDGE + sizey, HALO))),
    )

    level = bx // 2
    odd = bx % 2 == 1
    outward = 2 * PY * (2 * (bx % 2) - 1)
    direct = pick(odd, 3 - level, level)
    outer = jnp.logical_and(bx > 0, bx < rows - 1)
    relays_x = pick(odd, level, 3 - level) > 0
    relayed_from = pick(odd, 4 - level, level + 1)

    def detours(s):
        return jnp.logical_and(outer, s % 4 >= direct)

    def relays(s):
        return jnp.logical_and(relays_x, s % 4 >= relayed_from)

    my_column = by % COLUMNS
    upper = by >= COLUMNS
    crosses = jnp.logical_or(by == COLUMNS - 1, by == COLUMNS)
    relays_y = jnp.logical_not(crosses)
    across = pick(upper, 0, COLUMNS)
    end = pick(upper, COLUMNS, COLUMNS - 1)
    part = sizex // COLUMNS

    barrier = pltpu.get_barrier_semaphore()
    pl.semaphore_signal(barrier, inc=1, device_id={"st": 1 - core}, device_id_type=pl.DeviceIdType.MESH)
    for other in range(1, PY):
        near = bx * PY + lax.rem(by + other, PY)
        far = lax.rem(bx + other, rows) * PY + by
        pl.semaphore_signal(barrier, inc=1, device_id={"dom": near}, device_id_type=pl.DeviceIdType.MESH)
        pl.semaphore_signal(barrier, inc=1, device_id={"dom": far}, device_id_type=pl.DeviceIdType.MESH)

    def load(s):
        return pltpu.make_async_copy(states.at[s, 0], field.at[s, inx, iny], load_sem.at[s])

    def remote(src, dst, send_sem, recv_sem, target):
        return pltpu.make_async_remote_copy(
            src_ref=src,
            dst_ref=dst,
            send_sem=send_sem,
            recv_sem=recv_sem,
            device_id={"dom": target},
            device_id_type=pl.DeviceIdType.MESH,
        )

    class Exchange:
        def __init__(self, source, landing, box_x, box_y, sems):
            self.source, self.landing, self.box_x, self.box_y = source, landing, box_x, box_y
            self.send, self.recv, self.part_send, self.part_recv, self.relay_send, self.relay_recv = sems

        def face(self, s, link):
            _, target, _, taken, placed = links[link]
            return remote(
                self.source(s, taken), self.landing.at[s, placed[0], placed[1]],
                self.send.at[s, link], self.recv.at[s, link], target,
            )

        def face_by_relay(self, s, link):
            _, _, _, taken, _ = links[link]
            return remote(
                self.source(s, taken), self.box_x.at[s], self.send.at[s, link], self.relay_recv.at[s, 0], dom + outward
            )

        def hand_on_face(self, s, link):
            placed = links[link][4]
            return remote(
                self.box_x.at[s], self.landing.at[s, placed[0], placed[1]],
                self.relay_send.at[s, 0], self.recv.at[s, link], dom - outward // 2,
            )

        def piece(self, s, link, at):
            _, _, _, taken, placed = links[link]
            return remote(
                self.source(s, (pl.ds(at * part, part), taken[1])),
                self.landing.at[s, pl.ds(HALO + at * part, part), placed[1]],
                self.part_send.at[s, at], self.part_recv.at[s, at], bx * PY + across + at,
            )

        def piece_by_relay(self, s, link, at):
            taken = links[link][3]
            return remote(
                self.source(s, (pl.ds(at * part, part), taken[1])), self.box_y.at[s, :, pl.ds(0, HALO)],
                self.part_send.at[s, at], self.relay_recv.at[s, 1], bx * PY + across + at,
            )

        def hand_on_piece(self, s, link):
            placed = links[link][4]
            return remote(
                self.box_y.at[s, :, pl.ds(0, HALO)],
                self.landing.at[s, pl.ds(HALO + my_column * part, part), placed[1]],
                self.relay_send.at[s, 1], self.part_recv.at[s].at[my_column], bx * PY + end,
            )

        def for_faces(self, s, act, by_relay):
            for link in (0, 1):
                outermost = odd if link == 0 else jnp.logical_not(odd)
                turns = jnp.logical_and(outermost, detours(s))

                @pl.when(jnp.logical_and(links[link][0], jnp.logical_not(turns)))
                def _():
                    act(self.face(s, link))

                @pl.when(jnp.logical_and(links[link][0], turns))
                def _():
                    act(by_relay(s, link))
            for link, at in ((2, COLUMNS - 1), (3, COLUMNS)):
                @pl.when(jnp.logical_and(links[link][0], by != at))
                def _():
                    act(self.face(s, link))

                @pl.when(by == at)
                def _():
                    for piece in range(COLUMNS):
                        straight = piece == (0 if link == 2 else COLUMNS - 1)
                        act((self.piece if straight else self.piece_by_relay)(s, link, piece))

        def start(self, s):
            self.for_faces(s, lambda copy: copy.start(), self.face_by_relay)

        def wait_sent(self, s):
            self.for_faces(s, lambda copy: copy.wait_send(), self.face_by_relay)
            self.for_relays(s, None, lambda copy: copy.wait_send())

        def for_relays(self, s, arrived, act):
            for link, mine in ((0, odd), (1, jnp.logical_not(odd))):
                @pl.when(jnp.logical_and(mine, relays(s)))
                def _():
                    if arrived is not None:
                        arrived(self.face_by_relay(s, link))
                    act(self.hand_on_face(s, link))
            for link, mine in ((2, upper), (3, jnp.logical_not(upper))):
                @pl.when(jnp.logical_and(mine, relays_y))
                def _():
                    if arrived is not None:
                        arrived(self.piece_by_relay(s, link, 0))
                    act(self.hand_on_piece(s, link))

        def hand_on(self, s):
            self.for_relays(s, lambda copy: copy.wait_recv(), lambda copy: copy.start())

        def wait_landed(self, s):
            for link in (0, 1):
                @pl.when(links[link][2])
                def _():
                    self.face(s, link).wait_recv()
            for link, at in ((2, COLUMNS), (3, COLUMNS - 1)):
                @pl.when(jnp.logical_and(links[link][2], by != at))
                def _():
                    self.face(s, link).wait_recv()

                @pl.when(by == at)
                def _():
                    for piece in range(COLUMNS):
                        self.piece(s, link, piece).wait_recv()

    def from_first(s, taken):
        return first.at[s, pl.ds(HALO + taken[0].start, taken[0].size), pl.ds(EDGE + taken[1].start, taken[1].size)]

    exchange1 = Exchange(
        lambda s, taken: states.at[s, 0, taken[0], taken[1]], field, box_x1, box_y1,
        (send1, recv1, part_send1, part_recv1, relay_send1, relay_recv1),
    )
    exchange2 = Exchange(
        from_first, first, box_x2, box_y2, (send2, recv2, part_send2, part_recv2, relay_send2, relay_recv2)
    )

    def start_loads(s, carry):
        load(s).start()
        return carry

    load_potential = pltpu.make_async_copy(potential.at[0], diagonal, potential_sem)
    load_potential.start()
    lax.fori_loop(0, count, start_loads, 0)

    def clear(s, carry):
        for link in range(4):
            placed = links[link][4]

            @pl.when(jnp.logical_not(links[link][2]))
            def _():
                zero = jnp.zeros((placed[0].size, placed[1].size, sizez), jnp.float32)
                field[s, placed[0], placed[1], :] = zero
                first[s, placed[0], placed[1], :] = zero
        return carry

    pl.semaphore_wait(barrier, 1 + 2 * (PY - 1))

    def start_first(s, carry):
        exchange1.start(s)
        return carry

    lax.fori_loop(0, AHEAD, start_first, 0)
    lax.fori_loop(0, count, clear, 0)
    band[...] = band_matrix(sizez)
    load_potential.wait()
    diagonal[...] = 3.0 * SCALED[0] + (diagonal[...] - 36.0) / 32.0

    def apply(padded, s, put):
        inner = padded[s, inx, iny, :].reshape(sizex * sizey, sizez)
        along_z[...] = jnp.dot(
            inner, band[...], precision=HIGHEST, preferred_element_type=jnp.float32
        ).reshape(sizex, sizey, sizez)

        def plane(x, carry):
            total = diagonal[x] * padded[s, HALO + x, iny, :] + along_z[x]
            for k in range(1, HALO + 1):
                beside = padded[s, HALO + x + k, iny, :] + padded[s, HALO + x - k, iny, :]
                beside = beside + padded[s, HALO + x, pl.ds(EDGE + k, sizey), :]
                beside = beside + padded[s, HALO + x, pl.ds(EDGE - k, sizey), :]
                total = total + SCALED[k] * beside
            put(x, total)
            return carry

        lax.fori_loop(0, sizex, plane, 0)

    def first_step(s):
        load(s).wait()
        exchange1.wait_landed(s)

        def put(x, total):
            first[s, HALO + x, iny, :] = total

        apply(field, s, put)
        exchange2.start(s)

    def to_mate(s):
        return pltpu.make_async_remote_copy(
            src_ref=filtered.at[s, 0],
            dst_ref=mate.at[s],
            send_sem=mate_send.at[s],
            recv_sem=mate_recv.at[s],
            device_id={"st": 1 - core},
            device_id_type=pl.DeviceIdType.MESH,
        )

    def second_step(s):
        exchange2.wait_landed(s)

        def put(x, total):
            filtered[s, 0, x] = 2.0 * total - field[s, HALO + x, iny, :]

        apply(first, s, put)
        to_mate(s).start()

    gram_sum[...] = jnp.zeros_like(gram_sum)

    def gram_of(group):
        low, high = group * GROUP, (group + 1) * GROUP
        half = 8 * (high + low)
        total = partial.at[pl.ds(0, 2 * half)]
        total[...] = jnp.zeros_like(total)
        for s in range(low, high):
            to_mate(s).wait_recv()

        def flat(ref, first_state, last_state, x):
            return jnp.concatenate(
                [
                    ref[first_state:last_state, x + beyond, pl.ds(8 * tile, 8), :].reshape(-1, sizez)
                    for beyond in range(PLANES)
                    for tile in range(sizey // 8)
                ],
                axis=1,
            )

        def halves(values):
            upper_half = values.astype(jnp.bfloat16)
            return upper_half, (values - upper_half.astype(jnp.float32)).astype(jnp.bfloat16)

        def products(turn, carry):
            x = turn * PLANES
            own = halves(flat(filtered.at[:, 0], 0, high, x))
            new = halves(flat(mate, low, high, x))
            if low:
                old = halves(flat(mate, 0, low, x))
                left = jnp.concatenate([own[0], old[0], own[1], old[1]], axis=0)
            else:
                left = jnp.concatenate(own, axis=0)
            right = jnp.concatenate(
                [own[0][8 * low :], new[0], own[1][8 * low :], new[1]], axis=0
            )
            total[...] += lax.dot_general(
                left, right, (((1,), (1,)), ((), ())), preferred_element_type=jnp.float32
            )
            return carry

        lax.fori_loop(0, sizex // PLANES, products, 0)

        def iota(shape, dimension):
            return lax.broadcasted_iota(jnp.int32, shape, dimension)

        def left_state(index):
            index = index - half * (index >= half).astype(jnp.int32)
            own_state = index < 8 * high
            return (index - 8 * high * (index >= 8 * high).astype(jnp.int32)) // 8, own_state

        def right_state(index):
            index = index % (16 * GROUP)
            own_state = index < 8 * GROUP
            return low + (index % (8 * GROUP)) // 8, own_state

        def lane_of(state, own_state):
            own_state = own_state.astype(jnp.int32)
            return state + count * (own_state * core + (1 - own_state) * (1 - core))

        def dot(left, right):
            return jnp.dot(left, right, precision=HIGHEST, preferred_element_type=jnp.float32)

        wide = 32 * GROUP
        equal_rows = iota((2 * half, wide), 0) % 8 == iota((2 * half, wide), 1) % 8
        values = jnp.where(equal_rows, total[...], 0.0)
        state, own_state = left_state(iota((count, 2 * half), 1))
        rows_of = jnp.logical_and(own_state, state == iota((count, 2 * half), 0)).astype(jnp.float32)
        lane = lane_of(*right_state(iota((wide, 128), 0)))
        lanes_of = (lane == iota((wide, 128), 1)).astype(jnp.float32)
        gram_sum[...] += dot(dot(rows_of, values), lanes_of)
        if low:
            state, own_state = right_state(iota((count, wide), 1))
            rows_of = jnp.logical_and(own_state, state == iota((count, wide), 0)).astype(jnp.float32)
            state, own_state = left_state(iota((2 * half, 128), 0))
            lanes_of = jnp.logical_and(
                state < low, lane_of(state, own_state) == iota((2 * half, 128), 1)
            ).astype(jnp.float32)
            turned = lax.dot_general(
                rows_of, values, (((1,), (1,)), ((), ())), precision=HIGHEST, preferred_element_type=jnp.float32
            )
            gram_sum[...] += dot(turned, lanes_of)

    def when_state(s, act):
        @pl.when(jnp.logical_and(s >= 0, s < count))
        def _():
            act(s)

    for early in range(RELAYED):
        exchange1.hand_on(early)
    groups = count // GROUP

    def turn(t, carry):
        when_state(t - RELAYED2, exchange2.hand_on)
        when_state(t + RELAYED, exchange1.hand_on)
        when_state(t + AHEAD, exchange1.start)
        when_state(t, first_step)
        when_state(t - BEHIND, second_step)
        for group in range(groups - 1):
            @pl.when(t - BEHIND == (group + 1) * GROUP)
            def _():
                gram_of(group)
        return carry

    lax.fori_loop(0, count + BEHIND, turn, 0)
    gram_of(groups - 1)

    mine = gram_sum[...]

    def sum_over(stage, buffer, at, position, value):
        buffer[at] = value

        def copy(other):
            return pltpu.make_async_remote_copy(
                src_ref=buffer.at[at],
                dst_ref=buffer.at[at],
                send_sem=sum_send.at[stage, other],
                recv_sem=sum_recv.at[stage, at],
                device_id={"dom": position(lax.rem(at + other, PY))},
                device_id_type=pl.DeviceIdType.MESH,
            )

        def arriving(other):
            source = lax.rem(at + other, PY)
            return pltpu.make_async_remote_copy(
                src_ref=buffer.at[source],
                dst_ref=buffer.at[source],
                send_sem=sum_send.at[stage, other],
                recv_sem=sum_recv.at[stage, source],
                device_id={"dom": position(source)},
                device_id_type=pl.DeviceIdType.MESH,
            )

        for other in range(1, PY):
            copy(other).start()
        for other in range(1, PY):
            arriving(other).wait_recv()
        for other in range(1, PY):
            copy(other).wait_send()
        total = buffer[0]
        for other in range(1, PY):
            total = total + buffer[other]
        return total

    row_sum = sum_over(0, sums_y, by, lambda at: bx * PY + at, mine)
    whole = sum_over(1, sums_x, bx, lambda at: at * PY + by, row_sum)
    cells = lax.axis_size("dom") * sizex * sizey * sizez
    gram[...] = whole[:, : gram.shape[1]] / cells

    def finish(s, carry):
        exchange1.wait_sent(s)
        exchange2.wait_sent(s)
        to_mate(s).wait_send()
        return carry

    lax.fori_loop(0, count, finish, 0)


def on_device(states, potential):
    count, _, sizex, sizey, sizez = states.shape
    padded = (count, sizex + 2 * HALO, sizey + 2 * EDGE, sizez)
    dma = pltpu.SemaphoreType.DMA
    return pl.pallas_call(
        kernel,
        out_shape=(
            jax.ShapeDtypeStruct(states.shape, jnp.float32),
            jax.ShapeDtypeStruct((count, 2 * count), jnp.float32),
        ),
        in_specs=[pl.BlockSpec(memory_space=pl.ANY), pl.BlockSpec(memory_space=pl.ANY)],
        out_specs=(pl.BlockSpec(memory_space=pltpu.VMEM), pl.BlockSpec(memory_space=pltpu.VMEM)),
        scratch_shapes=[
            pltpu.VMEM(padded, jnp.float32),
            pltpu.VMEM(padded, jnp.float32),
            pltpu.VMEM((count, sizex, sizey, sizez), jnp.float32),
            pltpu.VMEM((sizex, sizey, sizez), jnp.float32),
            pltpu.VMEM((sizex, sizey, sizez), jnp.float32),
            pltpu.VMEM((sizez, sizez), jnp.float32),
            pltpu.VMEM((16 * (2 * count - GROUP), 32 * GROUP), jnp.float32),
            pltpu.VMEM((count, 128), jnp.float32),
            pltpu.VMEM((PY, count, 128), jnp.float32),
            pltpu.VMEM((PY, count, 128), jnp.float32),
            pltpu.VMEM((count, HALO, sizey, sizez), jnp.float32),
            pltpu.VMEM((count, sizex // COLUMNS, 8, sizez), jnp.float32),
            pltpu.VMEM((count, HALO, sizey, sizez), jnp.float32),
            pltpu.VMEM((count, sizex // COLUMNS, 8, sizez), jnp.float32),
            dma,
            dma((count,)),
        ]
        + 2 * [
            dma((count, 4)),
            dma((count, 4)),
            dma((count, COLUMNS)),
            dma((count, COLUMNS)),
            dma((count, 2)),
            dma((count, 2)),
        ]
        + [
            dma((count,)),
            dma((count,)),
            dma((2, PY)),
            dma((2, PY)),
        ],
        compiler_params=pltpu.CompilerParams(
            collective_id=0, has_side_effects=True, vmem_limit_bytes=48 * 2**20
        ),
        name="chebyshev",
    )(states, potential)


def solution(mesh):
    in_specs = (P("st", "dom", None, None, None), P("dom", None, None, None))
    out_specs = (P("st", "dom", None, None, None), P("st", None))
    return jax.shard_map(
        on_device, mesh=mesh, in_specs=in_specs, out_specs=out_specs, check_vma=False
    )
```

```python
import functools

import jax
import jax.numpy as jnp
from jax import lax
from jax.experimental import pallas as pl
from jax.experimental.pallas import tpu as pltpu
from jax.sharding import PartitionSpec as P

COEFFS = (
    -5369.0 / 1800.0,
    12.0 / 7.0,
    -15.0 / 56.0,
    10.0 / 189.0,
    -1.0 / 112.0,
    2.0 / 1925.0,
    -1.0 / 16632.0,
)
SCALED = tuple(-2.0 * c / 32.0 for c in COEFFS)
PY = 8
COLUMNS = 4
AHEAD = 4
BEHIND = 4
RELAYED2 = 2
GROUP = 4
PLANES = 8
RELAYED = 2
HALO = 6
EDGE = 8
HIGHEST = lax.Precision.HIGHEST


def band_matrix(size):
    row = lax.broadcasted_iota(jnp.int32, (size, size), 0)
    column = lax.broadcasted_iota(jnp.int32, (size, size), 1)
    distance = jnp.abs(row - column)
    band = jnp.zeros((size, size), jnp.float32)
    for offset in range(1, HALO + 1):
        band = jnp.where(distance == offset, SCALED[offset], band)
    return band


def halves(values):
    upper = values.astype(jnp.bfloat16)
    return upper, (values - upper.astype(jnp.float32)).astype(jnp.bfloat16)


def pick(chosen, yes, no):
    chosen = chosen.astype(jnp.int32)
    return chosen * yes + (1 - chosen) * no


def kernel(
    states, potential, filtered, gram,
    field, first, mate, diagonal, along_z, band, partial, gram_sum, sums_y, sums_x,
    box_x1, box_y1, box_x2, box_y2,
    potential_sem, load_sem, send1, recv1, part_send1, part_recv1, relay_send1, relay_recv1,
    send2, recv2, part_send2, part_recv2, relay_send2, relay_recv2, mate_send, mate_recv, sum_send, sum_recv,
):
    count, _, sizex, sizey, sizez = states.shape
    rows = lax.axis_size("dom") // PY
    dom = lax.axis_index("dom")
    core = lax.axis_index("st")
    bx, by = dom // PY, dom % PY
    inx = pl.ds(HALO, sizex)
    iny = pl.ds(EDGE, sizey)

    links = (
        (bx < rows - 1, dom + PY, bx > 0, (pl.ds(sizex - HALO, HALO), pl.ds(0, sizey)), (pl.ds(0, HALO), iny)),
        (bx > 0, dom - PY, bx < rows - 1, (pl.ds(0, HALO), pl.ds(0, sizey)), (pl.ds(HALO + sizex, HALO), iny)),
        (by < PY - 1, dom + 1, by > 0, (pl.ds(0, sizex), pl.ds(sizey - HALO, HALO)), (inx, pl.ds(EDGE - HALO, HALO))),
        (by > 0, dom - 1, by < PY - 1, (pl.ds(0, sizex), pl.ds(0, HALO)), (inx, pl.ds(EDGE + sizey, HALO))),
    )

    level = bx // 2
    odd = bx % 2 == 1
    outward = 2 * PY * (2 * (bx % 2) - 1)
    direct = pick(odd, 3 - level, level)
    outer = jnp.logical_and(bx > 0, bx < rows - 1)
    relays_x = pick(odd, level, 3 - level) > 0
    relayed_from = pick(odd, 4 - level, level + 1)

    def place(s):
        return jnp.minimum(s, count - 1 - s) % 4

    def detours(s):
        return jnp.logical_and(outer, place(s) >= direct)

    def relays(s):
        return jnp.logical_and(relays_x, place(s) >= relayed_from)

    my_column = by % COLUMNS
    upper = by >= COLUMNS
    crosses = jnp.logical_or(by == COLUMNS - 1, by == COLUMNS)
    relays_y = jnp.logical_not(crosses)
    across = pick(upper, 0, COLUMNS)
    end = pick(upper, COLUMNS, COLUMNS - 1)
    part = sizex // COLUMNS

    barrier = pltpu.get_barrier_semaphore()
    pl.semaphore_signal(barrier, inc=1, device_id={"st": 1 - core}, device_id_type=pl.DeviceIdType.MESH)
    for other in range(1, PY):
        near = bx * PY + lax.rem(by + other, PY)
        far = lax.rem(bx + other, rows) * PY + by
        pl.semaphore_signal(barrier, inc=1, device_id={"dom": near}, device_id_type=pl.DeviceIdType.MESH)
        pl.semaphore_signal(barrier, inc=1, device_id={"dom": far}, device_id_type=pl.DeviceIdType.MESH)

    def load(s):
        return pltpu.make_async_copy(states.at[s, 0], field.at[s, inx, iny], load_sem.at[s])

    def remote(src, dst, send_sem, recv_sem, target):
        return pltpu.make_async_remote_copy(
            src_ref=src,
            dst_ref=dst,
            send_sem=send_sem,
            recv_sem=recv_sem,
            device_id={"dom": target},
            device_id_type=pl.DeviceIdType.MESH,
        )

    class Exchange:
        def __init__(self, source, landing, box_x, box_y, sems):
            self.source, self.landing, self.box_x, self.box_y = source, landing, box_x, box_y
            self.send, self.recv, self.part_send, self.part_recv, self.relay_send, self.relay_recv = sems

        def face(self, s, link):
            _, target, _, taken, placed = links[link]
            return remote(
                self.source(s, taken), self.landing.at[s, placed[0], placed[1]],
                self.send.at[s, link], self.recv.at[s, link], target,
            )

        def face_by_relay(self, s, link):
            _, _, _, taken, _ = links[link]
            return remote(
                self.source(s, taken), self.box_x.at[s], self.send.at[s, link], self.relay_recv.at[s, 0], dom + outward
            )

        def hand_on_face(self, s, link):
            placed = links[link][4]
            return remote(
                self.box_x.at[s], self.landing.at[s, placed[0], placed[1]],
                self.relay_send.at[s, 0], self.recv.at[s, link], dom - outward // 2,
            )

        def piece(self, s, link, at):
            _, _, _, taken, placed = links[link]
            return remote(
                self.source(s, (pl.ds(at * part, part), taken[1])),
                self.landing.at[s, pl.ds(HALO + at * part, part), placed[1]],
                self.part_send.at[s, at], self.part_recv.at[s, at], bx * PY + across + at,
            )

        def piece_by_relay(self, s, link, at):
            taken = links[link][3]
            return remote(
                self.source(s, (pl.ds(at * part, part), taken[1])), self.box_y.at[s, :, pl.ds(0, HALO)],
                self.part_send.at[s, at], self.relay_recv.at[s, 1], bx * PY + across + at,
            )

        def hand_on_piece(self, s, link):
            placed = links[link][4]
            return remote(
                self.box_y.at[s, :, pl.ds(0, HALO)],
                self.landing.at[s, pl.ds(HALO + my_column * part, part), placed[1]],
                self.relay_send.at[s, 1], self.part_recv.at[s].at[my_column], bx * PY + end,
            )

        def for_faces(self, s, act, by_relay):
            for link in (0, 1):
                outermost = odd if link == 0 else jnp.logical_not(odd)
                turns = jnp.logical_and(outermost, detours(s))

                @pl.when(jnp.logical_and(links[link][0], jnp.logical_not(turns)))
                def _():
                    act(self.face(s, link))

                @pl.when(jnp.logical_and(links[link][0], turns))
                def _():
                    act(by_relay(s, link))
            for link, at in ((2, COLUMNS - 1), (3, COLUMNS)):
                @pl.when(jnp.logical_and(links[link][0], by != at))
                def _():
                    act(self.face(s, link))

                @pl.when(by == at)
                def _():
                    for piece in range(COLUMNS):
                        straight = piece == (0 if link == 2 else COLUMNS - 1)
                        act((self.piece if straight else self.piece_by_relay)(s, link, piece))

        def start(self, s):
            self.for_faces(s, lambda copy: copy.start(), self.face_by_relay)

        def wait_sent(self, s):
            self.for_faces(s, lambda copy: copy.wait_send(), self.face_by_relay)
            self.for_relays(s, None, lambda copy: copy.wait_send())

        def for_relays(self, s, arrived, act):
            for link, mine in ((0, odd), (1, jnp.logical_not(odd))):
                @pl.when(jnp.logical_and(mine, relays(s)))
                def _():
                    if arrived is not None:
                        arrived(self.face_by_relay(s, link))
                    act(self.hand_on_face(s, link))
            for link, mine in ((2, upper), (3, jnp.logical_not(upper))):
                @pl.when(jnp.logical_and(mine, relays_y))
                def _():
                    if arrived is not None:
                        arrived(self.piece_by_relay(s, link, 0))
                    act(self.hand_on_piece(s, link))

        def hand_on(self, s):
            self.for_relays(s, lambda copy: copy.wait_recv(), lambda copy: copy.start())

        def wait_landed(self, s):
            for link in (0, 1):
                @pl.when(links[link][2])
                def _():
                    self.face(s, link).wait_recv()
            for link, at in ((2, COLUMNS), (3, COLUMNS - 1)):
                @pl.when(jnp.logical_and(links[link][2], by != at))
                def _():
                    self.face(s, link).wait_recv()

                @pl.when(by == at)
                def _():
                    for piece in range(COLUMNS):
                        self.piece(s, link, piece).wait_recv()

    def from_first(s, taken):
        return first.at[s, pl.ds(HALO + taken[0].start, taken[0].size), pl.ds(EDGE + taken[1].start, taken[1].size)]

    exchange1 = Exchange(
        lambda s, taken: states.at[s, 0, taken[0], taken[1]], field, box_x1, box_y1,
        (send1, recv1, part_send1, part_recv1, relay_send1, relay_recv1),
    )
    exchange2 = Exchange(
        from_first, first, box_x2, box_y2, (send2, recv2, part_send2, part_recv2, relay_send2, relay_recv2)
    )

    def start_loads(s, carry):
        load(s).start()
        return carry

    load_potential = pltpu.make_async_copy(potential.at[0], diagonal, potential_sem)
    load_potential.start()
    lax.fori_loop(0, count, start_loads, 0)

    def clear(s, carry):
        for link in range(4):
            placed = links[link][4]

            @pl.when(jnp.logical_not(links[link][2]))
            def _():
                zero = jnp.zeros((placed[0].size, placed[1].size, sizez), jnp.float32)
                field[s, placed[0], placed[1], :] = zero
                first[s, placed[0], placed[1], :] = zero
        return carry

    pl.semaphore_wait(barrier, 1 + 2 * (PY - 1))

    def start_first(s, carry):
        exchange1.start(s)
        return carry

    lax.fori_loop(0, AHEAD, start_first, 0)
    lax.fori_loop(0, count, clear, 0)
    once = jnp.concatenate(halves(band_matrix(sizez)), axis=1)
    band[...] = jnp.concatenate([once, once], axis=0)
    load_potential.wait()
    diagonal[...] = 3.0 * SCALED[0] + (diagonal[...] - 36.0) / 32.0

    def apply(padded, s, put):
        inner = halves(padded[s, inx, iny, :].reshape(sizex * sizey, sizez))
        along = jnp.dot(jnp.concatenate(inner, axis=1), band[...], preferred_element_type=jnp.float32)
        along_z[...] = (along[:, :sizez] + along[:, sizez:]).reshape(sizex, sizey, sizez)

        def plane(x, carry):
            total = diagonal[x] * padded[s, HALO + x, iny, :] + along_z[x]
            for k in range(1, HALO + 1):
                beside = padded[s, HALO + x + k, iny, :] + padded[s, HALO + x - k, iny, :]
                beside = beside + padded[s, HALO + x, pl.ds(EDGE + k, sizey), :]
                beside = beside + padded[s, HALO + x, pl.ds(EDGE - k, sizey), :]
                total = total + SCALED[k] * beside
            put(x, total)
            return carry

        lax.fori_loop(0, sizex, plane, 0)

    def first_step(s):
        load(s).wait()
        exchange1.wait_landed(s)

        def put(x, total):
            first[s, HALO + x, iny, :] = total

        apply(field, s, put)
        exchange2.start(s)

    def to_mate(s):
        return pltpu.make_async_remote_copy(
            src_ref=filtered.at[s, 0],
            dst_ref=mate.at[s],
            send_sem=mate_send.at[s],
            recv_sem=mate_recv.at[s],
            device_id={"st": 1 - core},
            device_id_type=pl.DeviceIdType.MESH,
        )

    def second_step(s):
        exchange2.wait_landed(s)

        def put(x, total):
            filtered[s, 0, x] = 2.0 * total - field[s, HALO + x, iny, :]

        apply(first, s, put)
        to_mate(s).start()

    gram_sum[...] = jnp.zeros_like(gram_sum)

    def gram_of(group):
        low, high = group * GROUP, (group + 1) * GROUP
        half = 8 * (high + low)
        total = partial.at[pl.ds(0, 2 * half)]
        total[...] = jnp.zeros_like(total)
        for s in range(low, high):
            to_mate(s).wait_recv()

        def flat(ref, first_state, last_state, x):
            return jnp.concatenate(
                [
                    ref[first_state:last_state, x + beyond, pl.ds(8 * tile, 8), :].reshape(-1, sizez)
                    for beyond in range(PLANES)
                    for tile in range(sizey // 8)
                ],
                axis=1,
            )

        def products(turn, carry):
            x = turn * PLANES
            own = halves(flat(filtered.at[:, 0], 0, high, x))
            new = halves(flat(mate, low, high, x))
            if low:
                old = halves(flat(mate, 0, low, x))
                left = jnp.concatenate([own[0], old[0], own[1], old[1]], axis=0)
            else:
                left = jnp.concatenate(own, axis=0)
            right = jnp.concatenate(
                [own[0][8 * low :], new[0], own[1][8 * low :], new[1]], axis=0
            )
            total[...] += lax.dot_general(
                left, right, (((1,), (1,)), ((), ())), preferred_element_type=jnp.float32
            )
            return carry

        lax.fori_loop(0, sizex // PLANES, products, 0)

        def iota(shape, dimension):
            return lax.broadcasted_iota(jnp.int32, shape, dimension)

        def left_state(index):
            own_state = index < 8 * high
            return (index - 8 * high * (index >= 8 * high).astype(jnp.int32)) // 8, own_state

        def right_state(index):
            index = index % (16 * GROUP)
            own_state = index < 8 * GROUP
            return low + (index % (8 * GROUP)) // 8, own_state

        def lane_of(state, own_state):
            own_state = own_state.astype(jnp.int32)
            return state + count * (own_state * core + (1 - own_state) * (1 - core))

        def dot(left, right):
            return jnp.dot(left, right, precision=HIGHEST, preferred_element_type=jnp.float32)

        wide = 32 * GROUP
        equal_rows = iota((half, wide), 0) % 8 == iota((half, wide), 1) % 8
        values = jnp.where(equal_rows, total[:half] + total[half:], 0.0)
        state, own_state = left_state(iota((count, half), 1))
        rows_of = jnp.logical_and(own_state, state == iota((count, half), 0)).astype(jnp.float32)
        lane = lane_of(*right_state(iota((wide, 128), 0)))
        lanes_of = (lane == iota((wide, 128), 1)).astype(jnp.float32)
        gram_sum[...] += dot(dot(rows_of, values), lanes_of)
        if low:
            state, own_state = right_state(iota((count, wide), 1))
            rows_of = jnp.logical_and(own_state, state == iota((count, wide), 0)).astype(jnp.float32)
            state, own_state = left_state(iota((half, 128), 0))
            lanes_of = jnp.logical_and(
                state < low, lane_of(state, own_state) == iota((half, 128), 1)
            ).astype(jnp.float32)
            turned = lax.dot_general(
                rows_of, values, (((1,), (1,)), ((), ())), precision=HIGHEST, preferred_element_type=jnp.float32
            )
            gram_sum[...] += dot(turned, lanes_of)

    def when_state(s, act):
        @pl.when(jnp.logical_and(s >= 0, s < count))
        def _():
            act(s)

    for early in range(RELAYED):
        exchange1.hand_on(early)
    groups = count // GROUP

    def turn(t, carry):
        when_state(t - RELAYED2, exchange2.hand_on)
        when_state(t + RELAYED, exchange1.hand_on)
        when_state(t + AHEAD, exchange1.start)
        when_state(t, first_step)
        when_state(t - BEHIND, second_step)
        for group in range(groups - 1):
            @pl.when(t - BEHIND == (group + 1) * GROUP)
            def _():
                gram_of(group)
        return carry

    lax.fori_loop(0, count + BEHIND, turn, 0)
    gram_of(groups - 1)

    mine = gram_sum[...]

    sent = []

    def sum_over(stage, buffer, at, position, value):
        buffer[at] = value

        def copy(other):
            return pltpu.make_async_remote_copy(
                src_ref=buffer.at[at],
                dst_ref=buffer.at[at],
                send_sem=sum_send.at[stage, other],
                recv_sem=sum_recv.at[stage, at],
                device_id={"dom": position(lax.rem(at + other, PY))},
                device_id_type=pl.DeviceIdType.MESH,
            )

        def arriving(other):
            source = lax.rem(at + other, PY)
            return pltpu.make_async_remote_copy(
                src_ref=buffer.at[source],
                dst_ref=buffer.at[source],
                send_sem=sum_send.at[stage, other],
                recv_sem=sum_recv.at[stage, source],
                device_id={"dom": position(source)},
                device_id_type=pl.DeviceIdType.MESH,
            )

        for other in range(1, PY):
            copy(other).start()
        for other in range(1, PY):
            arriving(other).wait_recv()
        sent.extend(copy(other) for other in range(1, PY))
        total = buffer[0]
        for other in range(1, PY):
            total = total + buffer[other]
        return total

    row_sum = sum_over(0, sums_y, by, lambda at: bx * PY + at, mine)
    whole = sum_over(1, sums_x, bx, lambda at: at * PY + by, row_sum)
    cells = lax.axis_size("dom") * sizex * sizey * sizez
    gram[...] = whole[:, : gram.shape[1]] / cells

    for copy in sent:
        copy.wait_send()

    def finish(s, carry):
        exchange1.wait_sent(s)
        exchange2.wait_sent(s)
        to_mate(s).wait_send()
        return carry

    lax.fori_loop(0, count, finish, 0)


def on_device(states, potential):
    count, _, sizex, sizey, sizez = states.shape
    padded = (count, sizex + 2 * HALO, sizey + 2 * EDGE, sizez)
    dma = pltpu.SemaphoreType.DMA
    return pl.pallas_call(
        kernel,
        out_shape=(
            jax.ShapeDtypeStruct(states.shape, jnp.float32),
            jax.ShapeDtypeStruct((count, 2 * count), jnp.float32),
        ),
        in_specs=[pl.BlockSpec(memory_space=pltpu.HBM), pl.BlockSpec(memory_space=pltpu.HBM)],
        out_specs=(pl.BlockSpec(memory_space=pltpu.VMEM), pl.BlockSpec(memory_space=pltpu.VMEM)),
        scratch_shapes=[
            pltpu.VMEM(padded, jnp.float32),
            pltpu.VMEM(padded, jnp.float32),
            pltpu.VMEM((count, sizex, sizey, sizez), jnp.float32),
            pltpu.VMEM((sizex, sizey, sizez), jnp.float32),
            pltpu.VMEM((sizex, sizey, sizez), jnp.float32),
            pltpu.VMEM((2 * sizez, 2 * sizez), jnp.bfloat16),
            pltpu.VMEM((16 * (2 * count - GROUP), 32 * GROUP), jnp.float32),
            pltpu.VMEM((count, 128), jnp.float32),
            pltpu.VMEM((PY, count, 128), jnp.float32),
            pltpu.VMEM((PY, count, 128), jnp.float32),
            pltpu.VMEM((count, HALO, sizey, sizez), jnp.float32),
            pltpu.VMEM((count, sizex // COLUMNS, 8, sizez), jnp.float32),
            pltpu.VMEM((count, HALO, sizey, sizez), jnp.float32),
            pltpu.VMEM((count, sizex // COLUMNS, 8, sizez), jnp.float32),
            dma,
            dma((count,)),
        ]
        + 2 * [
            dma((count, 4)),
            dma((count, 4)),
            dma((count, COLUMNS)),
            dma((count, COLUMNS)),
            dma((count, 2)),
            dma((count, 2)),
        ]
        + [
            dma((count,)),
            dma((count,)),
            dma((2, PY)),
            dma((2, PY)),
        ],
        compiler_params=pltpu.CompilerParams(
            collective_id=0, has_side_effects=True, vmem_limit_bytes=48 * 2**20
        ),
        name="chebyshev",
    )(states, potential)


def solution(mesh):
    in_specs = (P("st", "dom", None, None, None), P("dom", None, None, None))
    out_specs = (P("st", "dom", None, None, None), P("st", None))
    return jax.shard_map(
        on_device, mesh=mesh, in_specs=in_specs, out_specs=out_specs, check_vma=False
    )
```

```python
import functools

import jax
import jax.numpy as jnp
from jax import lax
from jax.experimental import pallas as pl
from jax.experimental.pallas import tpu as pltpu
from jax.sharding import PartitionSpec as P

COEFFS = (
    -5369.0 / 1800.0,
    12.0 / 7.0,
    -15.0 / 56.0,
    10.0 / 189.0,
    -1.0 / 112.0,
    2.0 / 1925.0,
    -1.0 / 16632.0,
)
SCALED = tuple(-2.0 * c / 32.0 for c in COEFFS)
PY = 8
COLUMNS = 4
AHEAD = 4
BEHIND = 4
RELAYED2 = 2
GROUP = 4
PLANES = 8
RELAYED = 2
HALO = 6
EDGE = 8
HIGHEST = lax.Precision.HIGHEST


def band_matrix(size):
    row = lax.broadcasted_iota(jnp.int32, (size, size), 0)
    column = lax.broadcasted_iota(jnp.int32, (size, size), 1)
    distance = jnp.abs(row - column)
    band = jnp.zeros((size, size), jnp.float32)
    for offset in range(1, HALO + 1):
        band = jnp.where(distance == offset, SCALED[offset], band)
    return band


def halves(values):
    upper = values.astype(jnp.bfloat16)
    return upper, (values - upper.astype(jnp.float32)).astype(jnp.bfloat16)


def pick(chosen, yes, no):
    chosen = chosen.astype(jnp.int32)
    return chosen * yes + (1 - chosen) * no


def kernel(
    states, potential, filtered, gram,
    field, first, mate, diagonal, along_z, band, partial, own_parts, mate_parts, gram_sum, sums_y, sums_x,
    box_x1, box_y1, box_x2, box_y2,
    potential_sem, load_sem, send1, recv1, relay_send1, relay_recv1, send2, recv2, relay_send2, relay_recv2, mate_send, mate_recv, sum_send, sum_recv,
):
    count, _, sizex, sizey, sizez = states.shape
    rows = lax.axis_size("dom") // PY
    dom = lax.axis_index("dom")
    core = lax.axis_index("st")
    bx, by = dom // PY, dom % PY
    inx = pl.ds(HALO, sizex)
    iny = pl.ds(EDGE, sizey)

    links = (
        (bx < rows - 1, dom + PY, bx > 0, (pl.ds(sizex - HALO, HALO), pl.ds(0, sizey)), (pl.ds(0, HALO), iny)),
        (bx > 0, dom - PY, bx < rows - 1, (pl.ds(0, HALO), pl.ds(0, sizey)), (pl.ds(HALO + sizex, HALO), iny)),
        (by < PY - 1, dom + 1, by > 0, (pl.ds(0, sizex), pl.ds(sizey - HALO, HALO)), (inx, pl.ds(EDGE - HALO, HALO))),
        (by > 0, dom - 1, by < PY - 1, (pl.ds(0, sizex), pl.ds(0, HALO)), (inx, pl.ds(EDGE + sizey, HALO))),
    )

    level = bx // 2
    odd = bx % 2 == 1
    outward = 2 * PY * (2 * (bx % 2) - 1)
    direct = pick(odd, 3 - level, level)
    outer = jnp.logical_and(bx > 0, bx < rows - 1)
    relays_x = pick(odd, level, 3 - level) > 0
    relayed_from = pick(odd, 4 - level, level + 1)

    def place(s):
        return jnp.minimum(s, count - 1 - s) % 4

    def detours(s):
        return jnp.logical_and(outer, place(s) >= direct)

    def relays(s):
        return jnp.logical_and(relays_x, place(s) >= relayed_from)

    my_column = by % COLUMNS
    upper = by >= COLUMNS
    crosses = jnp.logical_or(by == COLUMNS - 1, by == COLUMNS)
    relays_y = jnp.logical_not(crosses)
    across = pick(upper, 0, COLUMNS)
    end = pick(upper, COLUMNS, COLUMNS - 1)
    part = sizex // COLUMNS

    barrier = pltpu.get_barrier_semaphore()
    pl.semaphore_signal(barrier, inc=1, device_id={"st": 1 - core}, device_id_type=pl.DeviceIdType.MESH)
    for other in range(1, PY):
        near = bx * PY + lax.rem(by + other, PY)
        far = lax.rem(bx + other, rows) * PY + by
        pl.semaphore_signal(barrier, inc=1, device_id={"dom": near}, device_id_type=pl.DeviceIdType.MESH)
        pl.semaphore_signal(barrier, inc=1, device_id={"dom": far}, device_id_type=pl.DeviceIdType.MESH)

    load_states = pltpu.make_async_copy(states.at[:, 0], field.at[:, inx, iny], load_sem.at[0])

    def remote(src, dst, send_sem, recv_sem, target):
        return pltpu.make_async_remote_copy(
            src_ref=src,
            dst_ref=dst,
            send_sem=send_sem,
            recv_sem=recv_sem,
            device_id={"dom": target},
            device_id_type=pl.DeviceIdType.MESH,
        )

    def wait_for(ref, sem):
        pltpu.make_async_copy(ref, ref, sem).wait()

    neighbours = sum(link[0].astype(jnp.int32) for link in links)

    class Exchange:
        def __init__(self, source, landing, box_x, box_y, sems):
            self.source, self.landing, self.box_x, self.box_y = source, landing, box_x, box_y
            self.send, self.recv, self.relay_send, self.relay_recv = sems

        def face(self, s, link):
            _, target, _, taken, placed = links[link]
            return remote(
                self.source(s, taken), self.landing.at[s, placed[0], placed[1]],
                self.send.at[0], self.recv.at[s], target,
            )

        def face_by_relay(self, s, link):
            _, _, _, taken, _ = links[link]
            return remote(
                self.source(s, taken), self.box_x.at[s], self.send.at[0], self.relay_recv.at[s, 0], dom + outward
            )

        def hand_on_face(self, s, link):
            placed = links[link][4]
            return remote(
                self.box_x.at[s], self.landing.at[s, placed[0], placed[1]],
                self.relay_send.at[0], self.recv.at[s], dom - outward // 2,
            )

        def piece(self, s, link, at):
            _, _, _, taken, placed = links[link]
            return remote(
                self.source(s, (pl.ds(at * part, part), taken[1])),
                self.landing.at[s, pl.ds(HALO + at * part, part), placed[1]],
                self.send.at[0], self.recv.at[s], bx * PY + across + at,
            )

        def piece_by_relay(self, s, link, at):
            taken = links[link][3]
            return remote(
                self.source(s, (pl.ds(at * part, part), taken[1])), self.box_y.at[s, :, pl.ds(0, HALO)],
                self.send.at[0], self.relay_recv.at[s, 1], bx * PY + across + at,
            )

        def hand_on_piece(self, s, link):
            placed = links[link][4]
            return remote(
                self.box_y.at[s, :, pl.ds(0, HALO)],
                self.landing.at[s, pl.ds(HALO + my_column * part, part), placed[1]],
                self.relay_send.at[1], self.recv.at[s], bx * PY + end,
            )

        def for_faces(self, s, act, by_relay):
            for link in (0, 1):
                outermost = odd if link == 0 else jnp.logical_not(odd)
                turns = jnp.logical_and(outermost, detours(s))

                @pl.when(jnp.logical_and(links[link][0], jnp.logical_not(turns)))
                def _():
                    act(self.face(s, link))

                @pl.when(jnp.logical_and(links[link][0], turns))
                def _():
                    act(by_relay(s, link))
            for link, at in ((2, COLUMNS - 1), (3, COLUMNS)):
                @pl.when(jnp.logical_and(links[link][0], by != at))
                def _():
                    act(self.face(s, link))

                @pl.when(by == at)
                def _():
                    for piece in range(COLUMNS):
                        straight = piece == (0 if link == 2 else COLUMNS - 1)
                        act((self.piece if straight else self.piece_by_relay)(s, link, piece))

        def start(self, s):
            self.for_faces(s, lambda copy: copy.start(), self.face_by_relay)

        def wait_sent(self):
            for faces in (2, 3, 4):
                @pl.when(neighbours == faces)
                def _():
                    wait_for(self.landing.at[:, pl.ds(0, faces * HALO), iny], self.send.at[0])
            for share in (1, 2, 3):
                @pl.when(jnp.logical_and(relays_x, relayed_from == 4 - share))
                def _():
                    wait_for(self.box_x.at[pl.ds(0, count * share // 4)], self.relay_send.at[0])

            @pl.when(relays_y)
            def _():
                wait_for(self.box_y.at[:, :, pl.ds(0, HALO)], self.relay_send.at[1])

        def for_relays(self, s, arrived, act):
            for link, mine in ((0, odd), (1, jnp.logical_not(odd))):
                @pl.when(jnp.logical_and(mine, relays(s)))
                def _():
                    arrived(self.face_by_relay(s, link))
                    act(self.hand_on_face(s, link))
            for link, mine in ((2, upper), (3, jnp.logical_not(upper))):
                @pl.when(jnp.logical_and(mine, relays_y))
                def _():
                    arrived(self.piece_by_relay(s, link, 0))
                    act(self.hand_on_piece(s, link))

        def hand_on(self, s):
            self.for_relays(s, lambda copy: copy.wait_recv(), lambda copy: copy.start())

        def wait_landed(self, s):
            for faces in (2, 3, 4):
                @pl.when(neighbours == faces)
                def _():
                    wait_for(self.landing.at[s, pl.ds(0, faces * HALO), iny], self.recv.at[s])

    def from_first(s, taken):
        return first.at[s, pl.ds(HALO + taken[0].start, taken[0].size), pl.ds(EDGE + taken[1].start, taken[1].size)]

    exchange1 = Exchange(
        lambda s, taken: states.at[s, 0, taken[0], taken[1]], field, box_x1, box_y1,
        (send1, recv1, relay_send1, relay_recv1),
    )
    exchange2 = Exchange(
        from_first, first, box_x2, box_y2, (send2, recv2, relay_send2, relay_recv2)
    )

    load_states.start()
    load_potential = pltpu.make_async_copy(potential.at[0], diagonal, potential_sem)
    load_potential.start()

    def clear(s, carry):
        for link in range(4):
            placed = links[link][4]

            @pl.when(jnp.logical_not(links[link][2]))
            def _():
                zero = jnp.zeros((placed[0].size, placed[1].size, sizez), jnp.float32)
                field[s, placed[0], placed[1], :] = zero
                first[s, placed[0], placed[1], :] = zero
        return carry

    pl.semaphore_wait(barrier, 1 + 2 * (PY - 1))

    def start_first(s, carry):
        exchange1.start(s)
        return carry

    lax.fori_loop(0, AHEAD, start_first, 0)
    lax.fori_loop(0, count, clear, 0)
    once = jnp.concatenate(halves(band_matrix(sizez)), axis=1)
    band[...] = jnp.concatenate([once, once], axis=0)
    load_potential.wait()
    load_states.wait()
    diagonal[...] = 3.0 * SCALED[0] + (diagonal[...] - 36.0) / 32.0

    def apply(padded, s, put):
        inner = halves(padded[s, inx, iny, :].reshape(sizex * sizey, sizez))
        along = jnp.dot(jnp.concatenate(inner, axis=1), band[...], preferred_element_type=jnp.float32)
        along_z[...] = (along[:, :sizez] + along[:, sizez:]).reshape(sizex, sizey, sizez)

        def plane(x, carry):
            total = diagonal[x] * padded[s, HALO + x, iny, :] + along_z[x]
            for k in range(1, HALO + 1):
                beside = padded[s, HALO + x + k, iny, :] + padded[s, HALO + x - k, iny, :]
                beside = beside + padded[s, HALO + x, pl.ds(EDGE + k, sizey), :]
                beside = beside + padded[s, HALO + x, pl.ds(EDGE - k, sizey), :]
                total = total + SCALED[k] * beside
            put(x, total)
            return carry

        lax.fori_loop(0, sizex, plane, 0)

    def first_step(s):
        exchange1.wait_landed(s)

        def put(x, total):
            first[s, HALO + x, iny, :] = total

        apply(field, s, put)
        exchange2.start(s)

    def to_mate(s):
        return pltpu.make_async_remote_copy(
            src_ref=filtered.at[s, 0],
            dst_ref=mate.at[s],
            send_sem=mate_send.at[0],
            recv_sem=mate_recv.at[s // GROUP],
            device_id={"st": 1 - core},
            device_id_type=pl.DeviceIdType.MESH,
        )

    def second_step(s):
        exchange2.wait_landed(s)

        def put(x, total):
            filtered[s, 0, x] = 2.0 * total - field[s, HALO + x, iny, :]

        apply(first, s, put)
        to_mate(s).start()

    gram_sum[...] = jnp.zeros_like(gram_sum)

    def gram_of(group):
        low, high = group * GROUP, (group + 1) * GROUP
        half = 8 * (high + low)
        total = partial.at[pl.ds(0, 2 * half)]
        total[...] = jnp.zeros_like(total)
        wait_for(mate.at[pl.ds(low, GROUP)], mate_recv.at[group])

        def flat(ref, first_state, last_state, x):
            return jnp.concatenate(
                [
                    ref[first_state:last_state, x + beyond, pl.ds(8 * tile, 8), :].reshape(-1, sizez)
                    for beyond in range(PLANES)
                    for tile in range(sizey // 8)
                ],
                axis=1,
            )

        def products(turn, carry):
            x = turn * PLANES
            new_rows = pl.ds(8 * low, 8 * (high - low))
            own = halves(flat(filtered.at[:, 0], low, high, x))
            new = halves(flat(mate, low, high, x))
            for kept, values in ((own_parts, own), (mate_parts, new)):
                for which in (0, 1):
                    kept[which, turn, new_rows, :] = values[which]
            left = []
            for which in (0, 1):
                if low:
                    left.append(own_parts[which, turn, pl.ds(0, 8 * low), :])
                left.append(own[which])
                if low:
                    left.append(mate_parts[which, turn, pl.ds(0, 8 * low), :])
            right = jnp.concatenate([own[0], new[0], own[1], new[1]], axis=0)
            total[...] += lax.dot_general(
                jnp.concatenate(left, axis=0), right, (((1,), (1,)), ((), ())), preferred_element_type=jnp.float32
            )
            return carry

        lax.fori_loop(0, sizex // PLANES, products, 0)

        def iota(shape, dimension):
            return lax.broadcasted_iota(jnp.int32, shape, dimension)

        def left_state(index):
            own_state = index < 8 * high
            return (index - 8 * high * (index >= 8 * high).astype(jnp.int32)) // 8, own_state

        def right_state(index):
            index = index % (16 * GROUP)
            own_state = index < 8 * GROUP
            return low + (index % (8 * GROUP)) // 8, own_state

        def lane_of(state, own_state):
            own_state = own_state.astype(jnp.int32)
            return state + count * (own_state * core + (1 - own_state) * (1 - core))

        def dot(left, right):
            return jnp.dot(left, right, precision=HIGHEST, preferred_element_type=jnp.float32)

        wide = 32 * GROUP
        equal_rows = iota((half, wide), 0) % 8 == iota((half, wide), 1) % 8
        values = jnp.where(equal_rows, total[:half] + total[half:], 0.0)
        state, own_state = left_state(iota((count, half), 1))
        rows_of = jnp.logical_and(own_state, state == iota((count, half), 0)).astype(jnp.float32)
        lane = lane_of(*right_state(iota((wide, 128), 0)))
        lanes_of = (lane == iota((wide, 128), 1)).astype(jnp.float32)
        gram_sum[...] += dot(dot(rows_of, values), lanes_of)
        if low:
            state, own_state = right_state(iota((count, wide), 1))
            rows_of = jnp.logical_and(own_state, state == iota((count, wide), 0)).astype(jnp.float32)
            state, own_state = left_state(iota((half, 128), 0))
            lanes_of = jnp.logical_and(
                state < low, lane_of(state, own_state) == iota((half, 128), 1)
            ).astype(jnp.float32)
            turned = lax.dot_general(
                rows_of, values, (((1,), (1,)), ((), ())), precision=HIGHEST, preferred_element_type=jnp.float32
            )
            gram_sum[...] += dot(turned, lanes_of)

    def when_state(s, act):
        @pl.when(jnp.logical_and(s >= 0, s < count))
        def _():
            act(s)

    for early in range(RELAYED):
        exchange1.hand_on(early)
    groups = count // GROUP

    def turn(t, carry):
        when_state(t - RELAYED2, exchange2.hand_on)
        when_state(t + RELAYED, exchange1.hand_on)
        when_state(t + AHEAD, exchange1.start)
        when_state(t, first_step)
        when_state(t - BEHIND, second_step)
        for group in range(groups - 1):
            @pl.when(t - BEHIND == (group + 1) * GROUP)
            def _():
                gram_of(group)
        return carry

    lax.fori_loop(0, count + BEHIND, turn, 0)
    gram_of(groups - 1)

    mine = gram_sum[...]

    def sum_over(stage, buffer, at, position, value):
        buffer[at] = value

        def copy(other):
            return pltpu.make_async_remote_copy(
                src_ref=buffer.at[at],
                dst_ref=buffer.at[at],
                send_sem=sum_send.at[stage],
                recv_sem=sum_recv.at[stage],
                device_id={"dom": position(lax.rem(at + other, PY))},
                device_id_type=pl.DeviceIdType.MESH,
            )

        for other in range(1, PY):
            copy(other).start()
        wait_for(buffer.at[pl.ds(1, PY - 1)], sum_recv.at[stage])
        total = buffer[0]
        for other in range(1, PY):
            total = total + buffer[other]
        return total

    row_sum = sum_over(0, sums_y, by, lambda at: bx * PY + at, mine)
    whole = sum_over(1, sums_x, bx, lambda at: at * PY + by, row_sum)
    cells = lax.axis_size("dom") * sizex * sizey * sizez
    gram[...] = whole[:, : gram.shape[1]] / cells

    for stage, buffer in enumerate((sums_y, sums_x)):
        wait_for(buffer.at[pl.ds(1, PY - 1)], sum_send.at[stage])
    exchange1.wait_sent()
    exchange2.wait_sent()
    wait_for(mate, mate_send.at[0])


def on_device(states, potential):
    count, _, sizex, sizey, sizez = states.shape
    padded = (count, sizex + 2 * HALO, sizey + 2 * EDGE, sizez)
    dma = pltpu.SemaphoreType.DMA
    return pl.pallas_call(
        kernel,
        out_shape=(
            jax.ShapeDtypeStruct(states.shape, jnp.float32),
            jax.ShapeDtypeStruct((count, 2 * count), jnp.float32),
        ),
        in_specs=[pl.BlockSpec(memory_space=pltpu.HBM), pl.BlockSpec(memory_space=pltpu.HBM)],
        out_specs=(pl.BlockSpec(memory_space=pltpu.VMEM), pl.BlockSpec(memory_space=pltpu.VMEM)),
        scratch_shapes=[
            pltpu.VMEM(padded, jnp.float32),
            pltpu.VMEM(padded, jnp.float32),
            pltpu.VMEM((count, sizex, sizey, sizez), jnp.float32),
            pltpu.VMEM((sizex, sizey, sizez), jnp.float32),
            pltpu.VMEM((sizex, sizey, sizez), jnp.float32),
            pltpu.VMEM((2 * sizez, 2 * sizez), jnp.bfloat16),
            pltpu.VMEM((16 * (2 * count - GROUP), 32 * GROUP), jnp.float32),
            pltpu.VMEM((2, sizex // PLANES, 8 * count, PLANES * sizey // 8 * sizez), jnp.bfloat16),
            pltpu.VMEM((2, sizex // PLANES, 8 * count, PLANES * sizey // 8 * sizez), jnp.bfloat16),
            pltpu.VMEM((count, 128), jnp.float32),
            pltpu.VMEM((PY, count, 128), jnp.float32),
            pltpu.VMEM((PY, count, 128), jnp.float32),
            pltpu.VMEM((count, HALO, sizey, sizez), jnp.float32),
            pltpu.VMEM((count, sizex // COLUMNS, 8, sizez), jnp.float32),
            pltpu.VMEM((count, HALO, sizey, sizez), jnp.float32),
            pltpu.VMEM((count, sizex // COLUMNS, 8, sizez), jnp.float32),
            dma,
            dma((1,)),
        ]
        + 2 * [dma((1,)), dma((count,)), dma((2,)), dma((count, 2))]
        + [dma((1,)), dma((count // GROUP,)), dma((2,)), dma((2,))],
        compiler_params=pltpu.CompilerParams(
            collective_id=0, has_side_effects=True, vmem_limit_bytes=48 * 2**20
        ),
        name="chebyshev",
    )(states, potential)


def solution(mesh):
    in_specs = (P("st", "dom", None, None, None), P("dom", None, None, None))
    out_specs = (P("st", "dom", None, None, None), P("st", None))
    return jax.shard_map(
        on_device, mesh=mesh, in_specs=in_specs, out_specs=out_specs, check_vma=False
    )
```

```python
import functools

import jax
import jax.numpy as jnp
from jax import lax
from jax.experimental import pallas as pl
from jax.experimental.pallas import tpu as pltpu
from jax.sharding import PartitionSpec as P

COEFFS = (
    -5369.0 / 1800.0,
    12.0 / 7.0,
    -15.0 / 56.0,
    10.0 / 189.0,
    -1.0 / 112.0,
    2.0 / 1925.0,
    -1.0 / 16632.0,
)
SCALED = tuple(-2.0 * c / 32.0 for c in COEFFS)
PY = 8
COLUMNS = 4
AHEAD = 3
BEHIND = 4
RELAYED2 = 2
GROUP = 4
PLANES = 8
RELAYED = 2
HALO = 6
EDGE = 8
HIGHEST = lax.Precision.HIGHEST


def band_matrix(size):
    row = lax.broadcasted_iota(jnp.int32, (size, size), 0)
    column = lax.broadcasted_iota(jnp.int32, (size, size), 1)
    distance = jnp.abs(row - column)
    band = jnp.zeros((size, size), jnp.float32)
    for offset in range(1, HALO + 1):
        band = jnp.where(distance == offset, SCALED[offset], band)
    return band


def halves(values):
    upper = values.astype(jnp.bfloat16)
    return upper, (values - upper.astype(jnp.float32)).astype(jnp.bfloat16)


def pick(chosen, yes, no):
    chosen = chosen.astype(jnp.int32)
    return chosen * yes + (1 - chosen) * no


def kernel(
    states, potential, filtered, gram,
    field, first, mate, diagonal, along_z, band, partial, own_parts, mate_parts, gram_sum, sums_y, sums_x,
    box_x1, box_y1, box_x2, box_y2,
    potential_sem, load_sem, send1, recv1, relay_send1, relay_recv1, send2, recv2, relay_send2, relay_recv2, mate_send, mate_recv, sum_send, sum_recv,
):
    count, _, sizex, sizey, sizez = states.shape
    rows = lax.axis_size("dom") // PY
    dom = lax.axis_index("dom")
    core = lax.axis_index("st")
    bx, by = dom // PY, dom % PY
    inx = pl.ds(HALO, sizex)
    iny = pl.ds(EDGE, sizey)

    links = (
        (bx < rows - 1, dom + PY, bx > 0, (pl.ds(sizex - HALO, HALO), pl.ds(0, sizey)), (pl.ds(0, HALO), iny)),
        (bx > 0, dom - PY, bx < rows - 1, (pl.ds(0, HALO), pl.ds(0, sizey)), (pl.ds(HALO + sizex, HALO), iny)),
        (by < PY - 1, dom + 1, by > 0, (pl.ds(0, sizex), pl.ds(sizey - HALO, HALO)), (inx, pl.ds(EDGE - HALO, HALO))),
        (by > 0, dom - 1, by < PY - 1, (pl.ds(0, sizex), pl.ds(0, HALO)), (inx, pl.ds(EDGE + sizey, HALO))),
    )

    level = bx // 2
    odd = bx % 2 == 1
    outward = 2 * PY * (2 * (bx % 2) - 1)
    direct = pick(odd, 3 - level, level)
    outer = jnp.logical_and(bx > 0, bx < rows - 1)
    relays_x = pick(odd, level, 3 - level) > 0
    relayed_from = pick(odd, 4 - level, level + 1)

    def place(s):
        return jnp.minimum(s, count - 1 - s) % 4

    def detours(s):
        return jnp.logical_and(outer, place(s) >= direct)

    def relays(s):
        return jnp.logical_and(relays_x, place(s) >= relayed_from)

    my_column = by % COLUMNS
    upper = by >= COLUMNS
    crosses = jnp.logical_or(by == COLUMNS - 1, by == COLUMNS)
    relays_y = jnp.logical_not(crosses)
    across = pick(upper, 0, COLUMNS)
    end = pick(upper, COLUMNS, COLUMNS - 1)
    part = sizex // COLUMNS

    barrier = pltpu.get_barrier_semaphore()
    pl.semaphore_signal(barrier, inc=1, device_id={"st": 1 - core}, device_id_type=pl.DeviceIdType.MESH)
    for other in range(1, PY):
        near = bx * PY + lax.rem(by + other, PY)
        far = lax.rem(bx + other, rows) * PY + by
        pl.semaphore_signal(barrier, inc=1, device_id={"dom": near}, device_id_type=pl.DeviceIdType.MESH)
        pl.semaphore_signal(barrier, inc=1, device_id={"dom": far}, device_id_type=pl.DeviceIdType.MESH)

    load_states = pltpu.make_async_copy(states.at[:, 0], field.at[:, inx, iny], load_sem.at[0])

    def remote(src, dst, send_sem, recv_sem, target):
        return pltpu.make_async_remote_copy(
            src_ref=src,
            dst_ref=dst,
            send_sem=send_sem,
            recv_sem=recv_sem,
            device_id={"dom": target},
            device_id_type=pl.DeviceIdType.MESH,
        )

    def wait_for(ref, sem):
        pltpu.make_async_copy(ref, ref, sem).wait()

    neighbours = sum(link[0].astype(jnp.int32) for link in links)

    class Exchange:
        def __init__(self, source, landing, box_x, box_y, sems):
            self.source, self.landing, self.box_x, self.box_y = source, landing, box_x, box_y
            self.send, self.recv, self.relay_send, self.relay_recv = sems

        def face(self, s, link):
            _, target, _, taken, placed = links[link]
            return remote(
                self.source(s, taken), self.landing.at[s, placed[0], placed[1]],
                self.send.at[0], self.recv.at[s], target,
            )

        def face_by_relay(self, s, link):
            _, _, _, taken, _ = links[link]
            return remote(
                self.source(s, taken), self.box_x.at[s], self.send.at[0], self.relay_recv.at[s, 0], dom + outward
            )

        def hand_on_face(self, s, link):
            placed = links[link][4]
            return remote(
                self.box_x.at[s], self.landing.at[s, placed[0], placed[1]],
                self.relay_send.at[0], self.recv.at[s], dom - outward // 2,
            )

        def piece(self, s, link, at):
            _, _, _, taken, placed = links[link]
            return remote(
                self.source(s, (pl.ds(at * part, part), taken[1])),
                self.landing.at[s, pl.ds(HALO + at * part, part), placed[1]],
                self.send.at[0], self.recv.at[s], bx * PY + across + at,
            )

        def piece_by_relay(self, s, link, at):
            taken = links[link][3]
            return remote(
                self.source(s, (pl.ds(at * part, part), taken[1])), self.box_y.at[s, :, pl.ds(0, HALO)],
                self.send.at[0], self.relay_recv.at[s, 1], bx * PY + across + at,
            )

        def hand_on_piece(self, s, link):
            placed = links[link][4]
            return remote(
                self.box_y.at[s, :, pl.ds(0, HALO)],
                self.landing.at[s, pl.ds(HALO + my_column * part, part), placed[1]],
                self.relay_send.at[1], self.recv.at[s], bx * PY + end,
            )

        def for_faces(self, s, act, by_relay):
            for link in (0, 1):
                outermost = odd if link == 0 else jnp.logical_not(odd)
                turns = jnp.logical_and(outermost, detours(s))

                @pl.when(jnp.logical_and(links[link][0], jnp.logical_not(turns)))
                def _():
                    act(self.face(s, link))

                @pl.when(jnp.logical_and(links[link][0], turns))
                def _():
                    act(by_relay(s, link))
            for link, at in ((2, COLUMNS - 1), (3, COLUMNS)):
                @pl.when(jnp.logical_and(links[link][0], by != at))
                def _():
                    act(self.face(s, link))

                @pl.when(by == at)
                def _():
                    for piece in range(COLUMNS):
                        straight = piece == (0 if link == 2 else COLUMNS - 1)
                        act((self.piece if straight else self.piece_by_relay)(s, link, piece))

        def start(self, s):
            self.for_faces(s, lambda copy: copy.start(), self.face_by_relay)

        def wait_sent(self):
            for faces in (2, 3, 4):
                @pl.when(neighbours == faces)
                def _():
                    wait_for(self.landing.at[:, pl.ds(0, faces * HALO), iny], self.send.at[0])
            for share in (1, 2, 3):
                @pl.when(jnp.logical_and(relays_x, relayed_from == 4 - share))
                def _():
                    wait_for(self.box_x.at[pl.ds(0, count * share // 4)], self.relay_send.at[0])

            @pl.when(relays_y)
            def _():
                wait_for(self.box_y.at[:, :, pl.ds(0, HALO)], self.relay_send.at[1])

        def for_relays(self, s, arrived, act):
            for link, mine in ((0, odd), (1, jnp.logical_not(odd))):
                @pl.when(jnp.logical_and(mine, relays(s)))
                def _():
                    arrived(self.face_by_relay(s, link))
                    act(self.hand_on_face(s, link))
            for link, mine in ((2, upper), (3, jnp.logical_not(upper))):
                @pl.when(jnp.logical_and(mine, relays_y))
                def _():
                    arrived(self.piece_by_relay(s, link, 0))
                    act(self.hand_on_piece(s, link))

        def hand_on(self, s):
            self.for_relays(s, lambda copy: copy.wait_recv(), lambda copy: copy.start())

        def wait_landed(self, s):
            for faces in (2, 3, 4):
                @pl.when(neighbours == faces)
                def _():
                    wait_for(self.landing.at[s, pl.ds(0, faces * HALO), iny], self.recv.at[s])

    def from_first(s, taken):
        return first.at[s, pl.ds(HALO + taken[0].start, taken[0].size), pl.ds(EDGE + taken[1].start, taken[1].size)]

    exchange1 = Exchange(
        lambda s, taken: states.at[s, 0, taken[0], taken[1]], field, box_x1, box_y1,
        (send1, recv1, relay_send1, relay_recv1),
    )
    exchange2 = Exchange(
        from_first, first, box_x2, box_y2, (send2, recv2, relay_send2, relay_recv2)
    )

    load_states.start()
    load_potential = pltpu.make_async_copy(potential.at[0], diagonal, potential_sem)
    load_potential.start()

    def clear(s, carry):
        for link in range(4):
            placed = links[link][4]

            @pl.when(jnp.logical_not(links[link][2]))
            def _():
                zero = jnp.zeros((placed[0].size, placed[1].size, sizez), jnp.float32)
                field[s, placed[0], placed[1], :] = zero
                first[s, placed[0], placed[1], :] = zero
        return carry

    pl.semaphore_wait(barrier, 1 + 2 * (PY - 1))

    def start_first(s, carry):
        exchange1.start(s)
        return carry

    lax.fori_loop(0, AHEAD, start_first, 0)
    lax.fori_loop(0, count, clear, 0)
    once = jnp.concatenate(halves(band_matrix(sizez)), axis=1)
    band[...] = jnp.concatenate([once, once], axis=0)
    load_potential.wait()
    load_states.wait()
    diagonal[...] = 3.0 * SCALED[0] + (diagonal[...] - 36.0) / 32.0

    def apply(padded, s, put):
        inner = halves(padded[s, inx, iny, :].reshape(sizex * sizey, sizez))
        along = jnp.dot(jnp.concatenate(inner, axis=1), band[...], preferred_element_type=jnp.float32)
        along_z[...] = (along[:, :sizez] + along[:, sizez:]).reshape(sizex, sizey, sizez)

        def plane(x, carry):
            total = diagonal[x] * padded[s, HALO + x, iny, :] + along_z[x]
            for k in range(1, HALO + 1):
                beside = padded[s, HALO + x + k, iny, :] + padded[s, HALO + x - k, iny, :]
                beside = beside + padded[s, HALO + x, pl.ds(EDGE + k, sizey), :]
                beside = beside + padded[s, HALO + x, pl.ds(EDGE - k, sizey), :]
                total = total + SCALED[k] * beside
            put(x, total)
            return carry

        lax.fori_loop(0, sizex, plane, 0)

    def first_step(s):
        exchange1.wait_landed(s)

        def put(x, total):
            first[s, HALO + x, iny, :] = total

        apply(field, s, put)
        exchange2.start(s)

    def to_mate(s):
        return pltpu.make_async_remote_copy(
            src_ref=filtered.at[s, 0],
            dst_ref=mate.at[s],
            send_sem=mate_send.at[0],
            recv_sem=mate_recv.at[s // GROUP],
            device_id={"st": 1 - core},
            device_id_type=pl.DeviceIdType.MESH,
        )

    def second_step(s):
        exchange2.wait_landed(s)

        def put(x, total):
            filtered[s, 0, x] = 2.0 * total - field[s, HALO + x, iny, :]

        apply(first, s, put)
        to_mate(s).start()

    gram_sum[...] = jnp.zeros_like(gram_sum)

    def gram_of(group):
        low, high = group * GROUP, (group + 1) * GROUP
        half = 8 * (high + low)
        total = partial.at[pl.ds(0, 2 * half)]
        total[...] = jnp.zeros_like(total)
        wait_for(mate.at[pl.ds(low, GROUP)], mate_recv.at[group])

        def flat(ref, first_state, last_state, x):
            return jnp.concatenate(
                [
                    ref[first_state:last_state, x + beyond, pl.ds(8 * tile, 8), :].reshape(-1, sizez)
                    for beyond in range(PLANES)
                    for tile in range(sizey // 8)
                ],
                axis=1,
            )

        def products(turn, carry):
            x = turn * PLANES
            new_rows = pl.ds(8 * low, 8 * (high - low))
            own = halves(flat(filtered.at[:, 0], low, high, x))
            new = halves(flat(mate, low, high, x))
            for kept, values in ((own_parts, own), (mate_parts, new)):
                for which in (0, 1):
                    kept[which, turn, new_rows, :] = values[which]
            left = []
            for which in (0, 1):
                if low:
                    left.append(own_parts[which, turn, pl.ds(0, 8 * low), :])
                left.append(own[which])
                if low:
                    left.append(mate_parts[which, turn, pl.ds(0, 8 * low), :])
            right = jnp.concatenate([own[0], new[0], own[1], new[1]], axis=0)
            total[...] += lax.dot_general(
                jnp.concatenate(left, axis=0), right, (((1,), (1,)), ((), ())), preferred_element_type=jnp.float32
            )
            return carry

        lax.fori_loop(0, sizex // PLANES, products, 0)

        def iota(shape, dimension):
            return lax.broadcasted_iota(jnp.int32, shape, dimension)

        def left_state(index):
            own_state = index < 8 * high
            return (index - 8 * high * (index >= 8 * high).astype(jnp.int32)) // 8, own_state

        def right_state(index):
            index = index % (16 * GROUP)
            own_state = index < 8 * GROUP
            return low + (index % (8 * GROUP)) // 8, own_state

        def lane_of(state, own_state):
            own_state = own_state.astype(jnp.int32)
            return state + count * (own_state * core + (1 - own_state) * (1 - core))

        def dot(left, right):
            return jnp.dot(left, right, precision=HIGHEST, preferred_element_type=jnp.float32)

        wide = 32 * GROUP
        equal_rows = iota((half, wide), 0) % 8 == iota((half, wide), 1) % 8
        values = jnp.where(equal_rows, total[:half] + total[half:], 0.0)
        state, own_state = left_state(iota((count, half), 1))
        rows_of = jnp.logical_and(own_state, state == iota((count, half), 0)).astype(jnp.float32)
        lane = lane_of(*right_state(iota((wide, 128), 0)))
        lanes_of = (lane == iota((wide, 128), 1)).astype(jnp.float32)
        gram_sum[...] += dot(dot(rows_of, values), lanes_of)
        if low:
            state, own_state = right_state(iota((count, wide), 1))
            rows_of = jnp.logical_and(own_state, state == iota((count, wide), 0)).astype(jnp.float32)
            state, own_state = left_state(iota((half, 128), 0))
            lanes_of = jnp.logical_and(
                state < low, lane_of(state, own_state) == iota((half, 128), 1)
            ).astype(jnp.float32)
            turned = lax.dot_general(
                rows_of, values, (((1,), (1,)), ((), ())), precision=HIGHEST, preferred_element_type=jnp.float32
            )
            gram_sum[...] += dot(turned, lanes_of)

    def when_state(s, act):
        @pl.when(jnp.logical_and(s >= 0, s < count))
        def _():
            act(s)

    for early in range(RELAYED):
        exchange1.hand_on(early)
    groups = count // GROUP

    def turn(t, carry):
        when_state(t - RELAYED2, exchange2.hand_on)
        when_state(t + RELAYED, exchange1.hand_on)
        when_state(t + AHEAD, exchange1.start)
        when_state(t, first_step)
        when_state(t - BEHIND, second_step)
        for group in range(groups - 1):
            @pl.when(t - BEHIND == (group + 1) * GROUP)
            def _():
                gram_of(group)
        return carry

    lax.fori_loop(0, count + BEHIND, turn, 0)
    gram_of(groups - 1)

    mine = gram_sum[...]

    def sum_over(stage, buffer, at, position, value):
        buffer[at] = value

        def copy(other):
            return pltpu.make_async_remote_copy(
                src_ref=buffer.at[at],
                dst_ref=buffer.at[at],
                send_sem=sum_send.at[stage],
                recv_sem=sum_recv.at[stage],
                device_id={"dom": position(lax.rem(at + other, PY))},
                device_id_type=pl.DeviceIdType.MESH,
            )

        for other in range(1, PY):
            copy(other).start()
        wait_for(buffer.at[pl.ds(1, PY - 1)], sum_recv.at[stage])
        total = buffer[0]
        for other in range(1, PY):
            total = total + buffer[other]
        return total

    row_sum = sum_over(0, sums_y, by, lambda at: bx * PY + at, mine)
    whole = sum_over(1, sums_x, bx, lambda at: at * PY + by, row_sum)
    cells = lax.axis_size("dom") * sizex * sizey * sizez
    gram[...] = whole[:, : gram.shape[1]] / cells

    for stage, buffer in enumerate((sums_y, sums_x)):
        wait_for(buffer.at[pl.ds(1, PY - 1)], sum_send.at[stage])
    exchange1.wait_sent()
    exchange2.wait_sent()
    wait_for(mate, mate_send.at[0])


def on_device(states, potential):
    count, _, sizex, sizey, sizez = states.shape
    padded = (count, sizex + 2 * HALO, sizey + 2 * EDGE, sizez)
    dma = pltpu.SemaphoreType.DMA
    return pl.pallas_call(
        kernel,
        out_shape=(
            jax.ShapeDtypeStruct(states.shape, jnp.float32),
            jax.ShapeDtypeStruct((count, 2 * count), jnp.float32),
        ),
        in_specs=[pl.BlockSpec(memory_space=pltpu.HBM), pl.BlockSpec(memory_space=pltpu.HBM)],
        out_specs=(pl.BlockSpec(memory_space=pltpu.VMEM), pl.BlockSpec(memory_space=pltpu.VMEM)),
        scratch_shapes=[
            pltpu.VMEM(padded, jnp.float32),
            pltpu.VMEM(padded, jnp.float32),
            pltpu.VMEM((count, sizex, sizey, sizez), jnp.float32),
            pltpu.VMEM((sizex, sizey, sizez), jnp.float32),
            pltpu.VMEM((sizex, sizey, sizez), jnp.float32),
            pltpu.VMEM((2 * sizez, 2 * sizez), jnp.bfloat16),
            pltpu.VMEM((16 * (2 * count - GROUP), 32 * GROUP), jnp.float32),
            pltpu.VMEM((2, sizex // PLANES, 8 * count, PLANES * sizey // 8 * sizez), jnp.bfloat16),
            pltpu.VMEM((2, sizex // PLANES, 8 * count, PLANES * sizey // 8 * sizez), jnp.bfloat16),
            pltpu.VMEM((count, 128), jnp.float32),
            pltpu.VMEM((PY, count, 128), jnp.float32),
            pltpu.VMEM((PY, count, 128), jnp.float32),
            pltpu.VMEM((count, HALO, sizey, sizez), jnp.float32),
            pltpu.VMEM((count, sizex // COLUMNS, 8, sizez), jnp.float32),
            pltpu.VMEM((count, HALO, sizey, sizez), jnp.float32),
            pltpu.VMEM((count, sizex // COLUMNS, 8, sizez), jnp.float32),
            dma,
            dma((1,)),
        ]
        + 2 * [dma((1,)), dma((count,)), dma((2,)), dma((count, 2))]
        + [dma((1,)), dma((count // GROUP,)), dma((2,)), dma((2,))],
        compiler_params=pltpu.CompilerParams(
            collective_id=0, has_side_effects=True, vmem_limit_bytes=48 * 2**20
        ),
        name="chebyshev",
    )(states, potential)


def solution(mesh):
    in_specs = (P("st", "dom", None, None, None), P("dom", None, None, None))
    out_specs = (P("st", "dom", None, None, None), P("st", None))
    return jax.shard_map(
        on_device, mesh=mesh, in_specs=in_specs, out_specs=out_specs, check_vma=False
    )
```
